256 devices in a mesh: queue: 32 (over y_hi, z, core), mp: 8 (over y_lo, x).
Axes of the slice: x: 4, y: 4 (y_hi: 2, y_lo: 2; y = y_hi * 2 + y_lo), z: 8, core: 2. Of those that a mesh axis runs over, the one named last changes fastest.
Arguments:
- latents: bfloat16 [16384, 3072], P('queue', 'mp'), may hold values from -6 to 6
- step_index: int32 [64], P('queue'), may hold values from 1 to 50
- head_index: int32 [1], replicated, may hold values from 0 to 63
- band: int32 [24], P('mp'), may hold values from 1 to 4, as said below
- mod_table: bfloat16 [50, 2, 3072], replicated, may hold values from -3 to 3
- gate_table: bfloat16 [50, 3072], P(None, 'mp'), may hold values from -4 to 4
- qkv_weight: bfloat16 [3, 3072, 3072], P(None, None, 'mp')
- out_weight: bfloat16 [3072, 3072], P('mp'), may hold values from -0.109375 to 0.109375
Outputs:
- velocity: bfloat16 [16384, 3072], P('queue', 'mp')
- head_frame: bfloat16 [256, 3072], P('queue', 'mp')
The draws below stay inside these ranges and needn't reach their ends.
Inputs may be any that keep to these rules, and one draw needn't show every extreme that they name: band is at most 4 and equals it for some head.
All inputs are finite; a program needn't handle non-finite values.
Results may differ from the reference program's by a relative error of at most 0.03.
Values may be sent and summed in bfloat16 or wider, within the bound.
No kernel may reach another device: no remote copies, remote signals or barrier semaphores. Data moves between devices by JAX's collectives and lax.ppermute only.
A program may use at most 128 MiB of HBM per device.

```python
import jax
import jax.numpy as jnp
from jax import lax

D = 3072
HEADS = 24
HEAD_DIM = 128
STEPS = 50
F_DEV = 2
TOKF = 256
NF = 64
TOKENS = 16384
N_QUEUE = 32
N_MP = 8


def draw_band(key, part):
    key = jax.random.fold_in(key, 11)
    first, second = jax.random.split(key)
    values = jax.random.randint(first, (HEADS,), 1, 2 * F_DEV + 1)
    chosen = jax.random.randint(second, (), 0, HEADS)
    return jnp.where(jnp.arange(HEADS) == chosen, 2 * F_DEV, values).astype(jnp.int32)


def draw_qkv_weight(key, part):
    key = jax.random.fold_in(key, 23)
    first = jax.random.fold_in(key, 0)
    base = jax.random.normal(first, (3, D, D), jnp.float32) * D ** (-0.5)
    return base.astype(jnp.bfloat16)


def with_ends(entries, own_key, least, largest):
    shape = entries.shape
    place = [jax.random.randint(jax.random.fold_in(own_key, axis), (), 0, shape[axis]) for axis in range(len(shape))]
    entries = entries.at[tuple(place)].set(least)
    longest = shape.index(max(shape))
    place[longest] = (place[longest] + 1) % shape[longest]
    return entries.at[tuple(place)].set(largest)


def shard_levels(own_key, dims, cuts, smallest, top_value):
    factor_of, own = 1.0, jax.random.fold_in(own_key, 6)
    for dim, blocks in cuts:
        heights = jnp.exp(jax.random.uniform(jax.random.fold_in(own, dim), (blocks,), jnp.float32, smallest / len(cuts), top_value / len(cuts)))
        factor_of = factor_of * jnp.repeat(heights, dims[dim] // blocks).reshape([-1 if axis == dim else 1 for axis in range(len(dims))])
    return factor_of


def noise(own_key, extent, scale, limit, cuts=(), kind=jnp.bfloat16):
    loudness = shard_levels(own_key, extent, cuts, -0.22, 0.18) if cuts else 1.0
    array = jax.random.normal(own_key, extent, jnp.float32) * scale * loudness
    return jnp.minimum(jnp.maximum(array, -limit), limit).astype(kind)


def setup_inputs(seed: int = 0) -> dict:
    key_list = jax.random.split(jax.random.key(seed), 9)
    return {
        "latents": noise(key_list[0], (TOKENS, D), 1.0, 6.0, ((0, 32), (1, 8))),
        "step_index": with_ends(jax.random.randint(key_list[1], (NF,), 1, STEPS + 1), jax.random.fold_in(key_list[1], 1), 1, STEPS).astype(jnp.int32),
        "head_index": jax.random.randint(key_list[2], (1,), 0, NF).astype(jnp.int32),
        "band": draw_band(jax.random.fold_in(key_list[8], 71), 0),
        "mod_table": noise(key_list[4], (STEPS, 2, D), 0.5, 3.0),
        "gate_table": noise(key_list[5], (STEPS, D), 1.0, 4.0, ((1, 8),)),
        "qkv_weight": draw_qkv_weight(jax.random.fold_in(key_list[8], 71), 0),
        "out_weight": noise(key_list[7], (D, D), D ** -0.5, 0.109375, ((0, 8),)),
    }


def attend_head(items):
    qhead, khead, vhead, reach, position = items
    window = 2 * F_DEV
    offsets = list(range(-window, window + 1))
    keys = jnp.stack([jnp.roll(khead, -shift_by, 0) for shift_by in offsets], 1).astype(jnp.float32)
    values = jnp.stack([jnp.roll(vhead, -shift_by, 0) for shift_by in offsets], 1).astype(jnp.float32)
    seen_pos = jnp.stack([jnp.roll(position, -shift_by) for shift_by in offsets], 1)
    allowed = jnp.abs(seen_pos - position[:, None]) <= reach
    scores = jnp.einsum('ftd,fgsd->ftgs', qhead.astype(jnp.float32), keys) / jnp.sqrt(jnp.float32(HEAD_DIM))
    scores = jnp.where(allowed[:, None, :, None], scores, jnp.float32(-1e+30))
    top = lax.optimization_barrier(jnp.max(scores, axis=(2, 3), keepdims=True))
    expd = jnp.exp(scores - top)
    total = lax.optimization_barrier(jnp.sum(expd, axis=(2, 3)))
    weights = lax.optimization_barrier(expd.astype(jnp.bfloat16)).astype(jnp.float32)
    result = jnp.einsum('ftgs,fgsd->ftd', weights, values) / total[..., None]
    return result.astype(jnp.bfloat16)

def reference(latents, step_index, head_index, band, mod_table, gate_table, qkv_weight, out_weight):
    frames_all = F_DEV * N_QUEUE
    latent_f = latents.astype(jnp.float32).reshape(frames_all, TOKF, D)
    mean = lax.optimization_barrier(jnp.mean(latent_f, axis=-1, keepdims=True))
    var = lax.optimization_barrier(jnp.mean(jnp.square(latent_f - mean), axis=-1, keepdims=True))
    normed = (latent_f - mean) / jnp.sqrt(var + 1e-06)
    onehot = (step_index[:, None] == (jnp.arange(STEPS, dtype=jnp.int32) + 1)[None, :]).astype(jnp.bfloat16)
    modul = jnp.dot(onehot, mod_table.reshape(STEPS, 2 * D), preferred_element_type=jnp.float32).reshape(frames_all, 2, D)
    modulated = (normed * (1.0 + modul[:, 1][:, None, :]) + modul[:, 0][:, None, :]).astype(jnp.bfloat16)
    modulated = modulated.reshape(frames_all * TOKF, D)
    projections = []
    for which in range(3):
        made = jnp.dot(modulated, qkv_weight[which], preferred_element_type=jnp.float32).astype(jnp.bfloat16)
        projections.append(made.reshape(frames_all, TOKF, HEADS, HEAD_DIM).transpose(2, 0, 1, 3))
    head = head_index[0]
    position = jnp.mod(jnp.arange(frames_all, dtype=jnp.int32) - head, frames_all).astype(jnp.int32)
    positions = jnp.broadcast_to(position[None, :], (HEADS, frames_all))
    attended = lax.map(attend_head, (projections[0], projections[1], projections[2], band, positions))
    attended = attended.transpose(1, 2, 0, 3).reshape(frames_all * TOKF, D)
    group = D // N_MP
    projected = jnp.zeros((frames_all * TOKF, D), jnp.float32)
    for member in range(N_MP):
        partial_sum = jnp.dot(attended[:, member * group:(member + 1) * group], out_weight[member * group:(member + 1) * group], preferred_element_type=jnp.float32)
        projected = projected + partial_sum.astype(jnp.bfloat16).astype(jnp.float32)
    gate = jnp.dot(onehot, gate_table, preferred_element_type=jnp.float32)
    velocity = (latent_f + gate[:, None, :] * projected.reshape(frames_all, TOKF, D)).astype(jnp.bfloat16)
    level = step_index.astype(jnp.float32) / STEPS
    sigma = 3.0 * level / (1.0 + 2.0 * level)
    head_latent = lax.dynamic_index_in_dim(latent_f, head, 0, keepdims=False)
    head_velocity = lax.dynamic_index_in_dim(velocity, head, 0, keepdims=False).astype(jnp.float32)
    head_sigma = lax.dynamic_index_in_dim(sigma, head, 0, keepdims=False)
    head_frame = (head_latent - head_sigma * head_velocity).astype(jnp.bfloat16)
    return (velocity.reshape(frames_all * TOKF, D), head_frame)
```

```python
import functools

import jax
import jax.numpy as jnp
from jax import lax
from jax.experimental import pallas as pl
from jax.experimental.pallas import tpu as pltpu
from jax.sharding import PartitionSpec as P

STEPS = 50
EPS = 1e-06
BIG = 1e30
LOG2E = 1.4426950408889634
VMEM_LIMIT = 48 * 1024 * 1024


def ring(value, distance):
    return lax.ppermute(value, "mp", [(s, s // 4 * 4 + (s + distance) % 4) for s in range(8)])


def across(value):
    return lax.ppermute(value, "mp", [(s, s ^ 4) for s in range(8)])


def shifted(value, distance):
    count = lax.axis_size("queue")
    return lax.ppermute(value, "queue", [(s, (s + distance) % count) for s in range(count)])


def flipped(value, bit):
    return lax.ppermute(value, "queue", [(s, s ^ bit) for s in range(lax.axis_size("queue"))])


def vmem():
    return pl.BlockSpec(memory_space=pltpu.VMEM)


def smem():
    return pl.BlockSpec(memory_space=pltpu.SMEM)


def qkv_kernel(place, own, far, low, high, two_a, two_b, two_c, three_a, three_b, three_c, modul, weight, query, kv, opposite, made):
    rows, part = own.shape
    half = rows // 2
    width = weight.shape[1]
    first, second = three_a.shape[0], three_a.shape[0] + three_b.shape[0]
    opposite[:first] = three_a[...]
    opposite[first:second] = three_b[...]
    opposite[second:] = three_c[...]
    starts = [pl.multiple_of(place[i] * part, 128) for i in range(8)]
    chunk = 64
    for frame in range(2):
        if frame == 0:
            parts = [(own, 0), (far, 0), (low, 0), (high, 0), (two_a, 0), (two_a, half), (two_c, half), (opposite, 0)]
        else:
            parts = [(own, half), (far, half), (low, half), (high, half), (two_b, 0), (two_c, 0), (two_b, half), (opposite, half)]
        for at in range(0, half, chunk):
            def load(i):
                ref, base = parts[i]
                return ref[base + at : base + at + chunk, :].astype(jnp.float32)

            total = load(0)
            for i in range(1, 8):
                total = total + load(i)
            mean = jnp.sum(total, axis=1, keepdims=True) * (1.0 / width)
            square = jnp.square(load(0) - mean)
            for i in range(1, 8):
                square = square + jnp.square(load(i) - mean)
            var = jnp.sum(square, axis=1, keepdims=True) * (1.0 / width)
            inverse = lax.rsqrt(var + EPS)
            for i in range(8):
                columns = pl.ds(starts[i], part)
                shift = modul[frame, 0:1, columns].astype(jnp.float32)
                scale = modul[frame, 1:2, columns].astype(jnp.float32) + 1.0
                value = (load(i) - mean) * inverse * scale + shift
                made[frame * half + at : frame * half + at + chunk, columns] = value.astype(jnp.bfloat16)
        left = made[frame * half : (frame + 1) * half, :]
        for which in (1, 2, 0):
            result = jnp.dot(left, weight[which], preferred_element_type=jnp.float32).astype(jnp.bfloat16)
            for h in range(3):
                piece = result[:, h * 128 : (h + 1) * 128]
                if which == 0:
                    query[h, frame * half : (frame + 1) * half, :] = piece
                else:
                    kv[which - 1, h, frame * half : (frame + 1) * half, :] = piece


def attend_kernel(allowed, query, lower2, lower1, own, upper1, upper2, out, scores):
    head = pl.program_id(0)
    size = query.shape[2]
    tokf = query.shape[1] // 2
    factor = LOG2E / size**0.5
    frames = [(ref, f) for ref in (lower2, lower1, own, upper1, upper2) for f in range(2)]
    ones = jnp.ones((tokf, size), jnp.bfloat16)
    for f in range(2):
        q = query[0, f * tokf : (f + 1) * tokf, :]
        seen = [allowed[(head * 2 + f) * 9 + d] > 0 for d in range(9)]
        top = jnp.full((tokf, size), -BIG, jnp.float32)
        for d in range(9):
            ref, g = frames[f + d]
            k = ref[0, 0, g * tokf : (g + 1) * tokf, :]
            s = lax.dot_general(q, k, (((1,), (1,)), ((), ())), preferred_element_type=jnp.float32)
            scores[d] = s
            top = jnp.maximum(top, jnp.where(seen[d], jnp.maximum(s[:, :size], s[:, size:]), -BIG))
        largest = jnp.max(top, axis=1, keepdims=True) * factor
        total = jnp.zeros((tokf, 2 * size), jnp.float32)
        for d in range(9):
            ref, g = frames[f + d]
            v = jnp.concatenate([ref[1, 0, g * tokf : (g + 1) * tokf, :], ones], axis=1)
            base = jnp.where(seen[d], largest, BIG)
            weights = jnp.exp2(scores[d] * factor - base).astype(jnp.bfloat16)
            total = total + jnp.dot(weights, v, preferred_element_type=jnp.float32)
        out[f * tokf : (f + 1) * tokf, :] = (total[:, :size] / total[:, size:]).astype(jnp.bfloat16)


def project_kernel(slots, place, attended, weight, *outs):
    part = attended.shape[1]
    left = attended[...]
    for out, slot in zip(outs, slots):
        columns = pl.ds(pl.multiple_of(place[slot] * part, 128), part)
        out[...] = jnp.dot(left, weight[:, columns], preferred_element_type=jnp.float32).astype(jnp.bfloat16)


def project(place, attended, weight, slots):
    rows, part = attended.shape
    return pl.pallas_call(
        functools.partial(project_kernel, slots),
        out_shape=[jax.ShapeDtypeStruct((rows, part), jnp.bfloat16)] * len(slots),
        in_specs=[smem(), vmem(), vmem()],
        out_specs=[vmem()] * len(slots),
        compiler_params=pltpu.CompilerParams(vmem_limit_bytes=VMEM_LIMIT),
        cost_estimate=pl.CostEstimate(
            flops=2 * rows * part * part * len(slots), bytes_accessed=2 * part * (rows + part) * len(slots), transcendentals=0
        ),
    )(place, attended, weight)


def on_device(latents, step_index, head_index, band, mod_table, gate_table, qkv_weight, out_weight):
    rows, part = latents.shape
    frames = step_index.shape[0]
    tokf = rows // frames
    width = mod_table.shape[2]
    heads = band.shape[0]
    size = part // heads
    count = lax.axis_size("queue")
    me = lax.axis_index("queue")
    member = lax.axis_index("mp")
    frames_all = frames * count
    half = rows // 2
    x, y = member % 4, member // 4
    place = jnp.stack([yy * 4 + xx for yy, xx in (
        (y, x), (1 - y, x), (y, (x + 3) % 4), (y, (x + 1) % 4),
        (y, (x + 2) % 4), (1 - y, (x + 3) % 4), (1 - y, (x + 1) % 4), (1 - y, (x + 2) % 4),
    )]).astype(jnp.int32)

    cuts = (0, 176, 336, rows)
    far, low, high = across(latents), ring(latents, 1), ring(latents, -1)
    two_a = ring(jnp.concatenate([low[:half], far[:half]]), 1)
    two_b = ring(jnp.concatenate([high[half:], far[half:]]), -1)
    two_c = across(jnp.concatenate([low[half:], high[:half]]))
    far_low_top, far_low_bottom = two_a[half:], two_c[:half]
    far_high_top, far_high_bottom = two_c[half:], two_b[half:]
    three_a = ring(far_low_top[: cuts[1]], 1)
    three_b = across(jnp.concatenate([two_a[cuts[1] : half], two_b[: cuts[2] - half]]))
    three_c = ring(far_high_bottom[cuts[2] - half :], -1)

    modul = jnp.stack([lax.dynamic_index_in_dim(mod_table, step_index[f] - 1, 0, keepdims=False) for f in range(frames)])
    query, kv = pl.pallas_call(
        qkv_kernel,
        out_shape=[
            jax.ShapeDtypeStruct((heads, rows, size), jnp.bfloat16),
            jax.ShapeDtypeStruct((2, heads, rows, size), jnp.bfloat16),
        ],
        in_specs=[smem()] + [vmem()] * 12,
        out_specs=[vmem()] * 2,
        scratch_shapes=[pltpu.VMEM((rows, part), jnp.bfloat16), pltpu.VMEM((rows, width), jnp.bfloat16)],
        compiler_params=pltpu.CompilerParams(vmem_limit_bytes=VMEM_LIMIT),
        cost_estimate=pl.CostEstimate(flops=6 * rows * width * part, bytes_accessed=6 * width * part, transcendentals=0),
    )(place, latents, far, low, high, two_a, two_b, two_c, three_a, three_b, three_c, modul, qkv_weight)

    lower2, upper2 = shifted(kv, 2), shifted(kv, -2)
    partner = flipped(kv, 1)
    odd = me % 2 == 1
    passed = flipped(jnp.where(odd, lower2, upper2), 1)
    lower1 = jnp.where(odd, partner, passed)
    upper1 = jnp.where(odd, passed, partner)

    head = head_index[0]
    position = jnp.mod(me * frames + jnp.arange(frames, dtype=jnp.int32) - head, frames_all)
    offset = jnp.arange(-4, 5, dtype=jnp.int32)
    other = position[:, None] + offset[None, :]
    inside = (other >= 0) & (other < frames_all)
    near = jnp.abs(offset)[None, :] <= band[:, None]
    allowed = (inside[None, :, :] & near[:, None, :]).astype(jnp.int32).reshape(-1)

    block = pl.BlockSpec((2, 1, rows, size), lambda h: (0, h, 0, 0))
    attended = pl.pallas_call(
        attend_kernel,
        grid=(heads,),
        out_shape=jax.ShapeDtypeStruct((rows, part), jnp.bfloat16),
        in_specs=[smem(), pl.BlockSpec((1, rows, size), lambda h: (h, 0, 0))] + [block] * 5,
        out_specs=pl.BlockSpec((rows, size), lambda h: (0, h)),
        scratch_shapes=[pltpu.VMEM((9, tokf, tokf), jnp.float32)],
        compiler_params=pltpu.CompilerParams(vmem_limit_bytes=VMEM_LIMIT),
        cost_estimate=pl.CostEstimate(
            flops=8 * heads * rows * 9 * tokf * size, bytes_accessed=24 * heads * rows * size, transcendentals=heads * rows * 9 * tokf
        ),
    )(allowed, query, lower2, lower1, kv, upper1, upper2)

    (opp_far,) = project(place, attended, out_weight, (7,))
    to_low = ring(opp_far[: cuts[1]], -1)
    to_far = across(opp_far[cuts[1] : cuts[2]])
    to_high = ring(opp_far[cuts[2] :], 1)
    p_opp, p_far_low, p_far_high = project(place, attended, out_weight, (4, 5, 6))

    def added(*terms):
        total = terms[0].astype(jnp.float32)
        for term in terms[1:]:
            total = total + term.astype(jnp.float32)
        return total

    bf = jnp.bfloat16
    far_low_top = jnp.concatenate([added(p_far_low[: cuts[1]], to_low).astype(bf), p_far_low[cuts[1] : half]])
    far_high_bottom = jnp.concatenate([p_far_high[half : cuts[2]], added(p_far_high[cuts[2] :], to_high).astype(bf)])
    opp_top = jnp.concatenate([p_opp[: cuts[1]], added(p_opp[cuts[1] : half], to_far[: half - cuts[1]]).astype(bf)])
    opp_bottom = jnp.concatenate([added(p_opp[half : cuts[2]], to_far[half - cuts[1] :]).astype(bf), p_opp[cuts[2] :]])
    got_a = ring(jnp.concatenate([opp_top, far_low_top]), -1)
    got_b = ring(jnp.concatenate([opp_bottom, far_high_bottom]), 1)
    got_c = across(jnp.concatenate([p_far_low[half:], p_far_high[:half]]))
    p_own, p_far, p_low, p_high = project(place, attended, out_weight, (0, 1, 2, 3))
    sum_low = jnp.concatenate([added(p_low[:half], got_a[:half]), added(p_low[half:], got_c[:half])]).astype(bf)
    sum_high = jnp.concatenate([added(p_high[:half], got_c[half:]), added(p_high[half:], got_b[:half])]).astype(bf)
    sum_far = jnp.concatenate([added(p_far[:half], got_a[half:]), added(p_far[half:], got_b[half:])]).astype(bf)
    projected = added(p_own, across(sum_far), ring(sum_low, -1), ring(sum_high, 1))

    gate = jnp.stack([lax.dynamic_index_in_dim(gate_table, step_index[f] - 1, 0, keepdims=False) for f in range(frames)])
    own_latent = latents.astype(jnp.float32).reshape(frames, tokf, part)
    velocity = (own_latent + gate.astype(jnp.float32)[:, None, :] * projected.reshape(frames, tokf, part)).astype(bf)

    level = step_index.astype(jnp.float32) / STEPS
    sigma = 3.0 * level / (1.0 + 2.0 * level)
    owner = head // frames
    local_frame = jnp.mod(head, frames)
    head_latent = lax.dynamic_index_in_dim(own_latent, local_frame, 0, keepdims=False)
    head_velocity = lax.dynamic_index_in_dim(velocity, local_frame, 0, keepdims=False).astype(jnp.float32)
    head_sigma = lax.dynamic_index_in_dim(sigma, local_frame, 0, keepdims=False)
    held = (head_latent - head_sigma * head_velocity).astype(bf)
    holder = owner
    bit = count // 2
    while bit:
        n = held.shape[0] // 2
        side = (me & bit) != 0
        mine = jnp.where(side, held[n:], held[:n])
        got = flipped(jnp.where(side, held[:n], held[n:]), bit)
        held = jnp.where((holder & bit) == (me & bit), mine, got)
        bit //= 2
    return (velocity.reshape(rows, part), held)


def solution(mesh):
    placed = (
        P("queue", "mp"),
        P("queue"),
        P(),
        P("mp"),
        P(),
        P(None, "mp"),
        P(None, None, "mp"),
        P("mp", None),
    )
    return jax.shard_map(
        on_device,
        mesh=mesh,
        in_specs=placed,
        out_specs=(P("queue", "mp"), P("queue", "mp")),
        check_vma=False,
    )
```

```python
import functools

import jax
import jax.numpy as jnp
from jax import lax
from jax.experimental import pallas as pl
from jax.experimental.pallas import tpu as pltpu
from jax.sharding import PartitionSpec as P

STEPS = 50
EPS = 1e-06
BIG = 1e30
SEEN, WINDOW, HEAD, OWN_STEP, MARKS = 8, 68, 70, 73, 75
LOG2E = 1.4426950408889634
VMEM_LIMIT = 48 * 1024 * 1024
SMALL_LIMIT = 12 * 1024 * 1024


def ring(value, distance):
    return lax.ppermute(value, "mp", [(s, s // 4 * 4 + (s + distance) % 4) for s in range(8)])


def across(value):
    return lax.ppermute(value, "mp", [(s, s ^ 4) for s in range(8)])


def shifted(value, distance):
    count = lax.axis_size("queue")
    return lax.ppermute(value, "queue", [(s, (s + distance) % count) for s in range(count)])


def flipped(value, bit):
    return lax.ppermute(value, "queue", [(s, s ^ bit) for s in range(lax.axis_size("queue"))])


def vmem():
    return pl.BlockSpec(memory_space=pltpu.VMEM)


def anywhere():
    return pl.BlockSpec(memory_space=pl.ANY)


def smem():
    return pl.BlockSpec(memory_space=pltpu.SMEM)


def qkv_kernel(place, own_at, far, low, high, far_opp, two_a, two_b, two_c, modul, weight_at, kv, made, own, weight, sems):
    rows, part = own.shape
    half = rows // 2
    width = weight.shape[1]
    cut = two_a.shape[0] - half
    copies = [
        pltpu.make_async_copy(source, target, sems.at[i])
        for i, (source, target) in enumerate(((own_at, own), (weight_at.at[1], weight.at[0]), (weight_at.at[2], weight.at[1])))
    ]
    for copy in copies:
        copy.start()
    copies[0].wait()
    starts = [pl.multiple_of(place[i] * part, 128) for i in range(8)]
    chunk = 32
    for frame in range(2):
        for at in range(frame * half, (frame + 1) * half, chunk):
            parts = [
                (own, at), (far, at), (low, at), (high, at),
                (two_a, at) if at < half else (two_b, at - half),
                (two_a, half + at) if at < cut else (two_c, at - cut),
                (two_c, rows - cut + at) if at < rows - cut else (two_b, half + at - (rows - cut)),
                (far_opp, at),
            ]

            def load(i):
                ref, base = parts[i]
                return ref[base : base + chunk, :].astype(jnp.float32)

            total = load(0)
            for i in range(1, 8):
                total = total + load(i)
            mean = jnp.sum(total, axis=1, keepdims=True) * (1.0 / width)
            square = jnp.square(load(0) - mean)
            for i in range(1, 8):
                square = square + jnp.square(load(i) - mean)
            var = jnp.sum(square, axis=1, keepdims=True) * (1.0 / width)
            inverse = lax.rsqrt(var + EPS)
            for i in range(8):
                columns = pl.ds(starts[i], part)
                shift = modul[frame, 0:1, columns].astype(jnp.float32)
                scale = modul[frame, 1:2, columns].astype(jnp.float32) + 1.0
                value = (load(i) - mean) * inverse * scale + shift
                made[at : at + chunk, columns] = value.astype(jnp.bfloat16)
        left = made[frame * half : (frame + 1) * half, :]
        for which in range(2):
            if frame == 0:
                copies[1 + which].wait()
            result = jnp.dot(left, weight[which], preferred_element_type=jnp.float32).astype(jnp.bfloat16)
            for h in range(3):
                kv[which, h, frame * half : (frame + 1) * half, :] = result[:, h * 128 : (h + 1) * 128]


def query_kernel(made_at, weight_at, query, made, weight, sems):
    copies = [pltpu.make_async_copy(weight_at.at[0], weight, sems.at[0]), pltpu.make_async_copy(made_at, made, sems.at[1])]
    for copy in copies:
        copy.start()
    for copy in copies:
        copy.wait()
    result = jnp.dot(made[...], weight[...], preferred_element_type=jnp.float32).astype(jnp.bfloat16)
    for h in range(3):
        query[h] = result[:, h * 128 : (h + 1) * 128]


def attend_kernel(shape, allowed, query, *rest):
    blocks, first, last = shape
    keys, rest = rest[: len(blocks)], rest[len(blocks) :]
    if not first:
        top_in, sum_in, *rest = rest
    if last:
        out, scores = rest
    else:
        top_out, sum_out, scores = rest
    size = query.shape[2]
    tokf = query.shape[1] // 2
    factor = LOG2E / size**0.5
    ones = jnp.ones((tokf, size), jnp.bfloat16)
    for head, f in [(head, f) for head in range(query.shape[0]) for f in range(2)]:
        rows = slice(f * tokf, (f + 1) * tokf)
        q = query[head, rows, :]
        tiles = []
        for ref, slot in zip(keys, blocks):
            for g in range(2):
                if (slot, g, f) in ((0, 0, 1), (4, 1, 0)):
                    continue
                place = allowed[WINDOW + slot - 5] if slot >= 5 else slot
                tiles.append((ref, slice(g * tokf, (g + 1) * tokf), allowed[SEEN + (head * 2 + f) * 10 + place * 2 + g] > 0))
        top = jnp.full((tokf, size), -BIG, jnp.float32)
        for t, (ref, at, seen) in enumerate(tiles):
            s = lax.dot_general(q, ref[0, head, at, :], (((1,), (1,)), ((), ())), preferred_element_type=jnp.float32)
            scores[(head + f) % 2, t] = s
            top = jnp.maximum(top, jnp.where(seen, jnp.maximum(s[:, :size], s[:, size:]), -BIG))
        largest = jnp.broadcast_to(jnp.max(top, axis=1, keepdims=True) * factor, (tokf, size))
        total = jnp.zeros((tokf, 2 * size), jnp.float32)
        if not first:
            before = top_in[head, rows, :]
            largest = jnp.maximum(largest, before)
            fade = jnp.exp2(before - largest)
            total = sum_in[head, rows, :] * jnp.concatenate([fade, fade], axis=1)
        for t, (ref, at, seen) in enumerate(tiles):
            v = jnp.concatenate([ref[1, head, at, :], ones], axis=1)
            base = jnp.where(seen, largest, BIG)
            weights = jnp.concatenate(
                [jnp.exp2(scores[(head + f) % 2, t, :, i * size : (i + 1) * size] * factor - base) for i in range(2)], axis=1
            ).astype(jnp.bfloat16)
            total = total + jnp.dot(weights, v, preferred_element_type=jnp.float32)
        if last:
            out[rows, head * size : (head + 1) * size] = (total[:, :size] / total[:, size:]).astype(jnp.bfloat16)
        else:
            top_out[head, rows, :] = largest
            sum_out[head, rows, :] = total


def attend(blocks, allowed, query, keys, state=(), last=False):
    heads, rows, size = query.shape
    tokf = rows // 2
    if last:
        out_shape = jax.ShapeDtypeStruct((rows, heads * size), jnp.bfloat16)
    else:
        out_shape = [jax.ShapeDtypeStruct((heads, rows, n * size), jnp.float32) for n in (1, 2)]
    tiles = 4 * len(blocks)
    return pl.pallas_call(
        functools.partial(attend_kernel, (blocks, not state, last)),
        out_shape=out_shape,
        in_specs=[smem()] + [vmem()] * (1 + len(keys) + len(state)),
        out_specs=vmem() if last else [vmem()] * 2,
        scratch_shapes=[pltpu.VMEM((2, 2 * len(blocks), tokf, tokf), jnp.float32)],
        compiler_params=pltpu.CompilerParams(vmem_limit_bytes=SMALL_LIMIT),
        cost_estimate=pl.CostEstimate(
            flops=6 * heads * tiles * tokf * tokf * size, bytes_accessed=4 * tiles * tokf * size, transcendentals=heads * tiles * tokf * tokf
        ),
    )(allowed, query, *keys, *state)


def added(*terms):
    total = terms[0].astype(jnp.float32)
    for term in terms[1:]:
        total = total + term.astype(jnp.float32)
    return total


def product(place, slot, left, weight):
    part = weight.shape[0]
    columns = pl.ds(pl.multiple_of(place[slot] * part, 128), part)
    return jnp.dot(left, weight[:, columns], preferred_element_type=jnp.float32).astype(jnp.bfloat16)


def first_kernel(cut, place, attended, weight, far_opp, two_a, two_b, two_c):
    rows = attended.shape[0]
    half = rows // 2
    left = attended[...]
    far_opp[...] = product(place, 7, left, weight)
    opp, far_low, far_high = (product(place, slot, left, weight) for slot in (4, 5, 6))
    two_a[:half] = opp[:half]
    two_a[half:] = far_low[:cut]
    two_b[:half] = opp[half:]
    two_b[half:] = far_high[rows - cut :]
    two_c[: rows - cut] = far_low[cut:]
    two_c[rows - cut :] = far_high[: rows - cut]


def second_kernel(cut, place, attended, weight, got_opp, got_a, got_b, got_c, sum_far, sum_low, sum_high, own):
    rows = attended.shape[0]
    half = rows // 2
    bf = jnp.bfloat16
    left = attended[...]
    far, low, high = (product(place, slot, left, weight) for slot in (1, 2, 3))
    sum_far[:cut] = added(far[:cut], got_opp[:cut], got_a[half:]).astype(bf)
    sum_far[cut : rows - cut] = added(far[cut : rows - cut], got_opp[cut : rows - cut]).astype(bf)
    sum_far[rows - cut :] = added(far[rows - cut :], got_opp[rows - cut :], got_b[half:]).astype(bf)
    sum_low[:cut] = added(low[:cut], got_a[:cut]).astype(bf)
    sum_low[cut:half] = added(low[cut:half], got_a[cut:half], got_c[: half - cut]).astype(bf)
    sum_low[half:] = added(low[half:], got_c[half - cut : rows - cut]).astype(bf)
    sum_high[:half] = added(high[:half], got_c[rows - cut : rows - cut + half]).astype(bf)
    sum_high[half : rows - cut] = added(high[half : rows - cut], got_b[: half - cut], got_c[rows - cut + half :]).astype(bf)
    sum_high[rows - cut :] = added(high[rows - cut :], got_b[half - cut : half]).astype(bf)
    own[...] = product(place, 0, left, weight)


def summed(kernel, place, attended, weight, terms, heights):
    rows, part = attended.shape
    return pl.pallas_call(
        kernel,
        out_shape=[jax.ShapeDtypeStruct((height, part), jnp.bfloat16) for height in heights],
        in_specs=[smem()] + [vmem()] * (2 + len(terms)),
        out_specs=[vmem()] * len(heights),
        compiler_params=pltpu.CompilerParams(vmem_limit_bytes=SMALL_LIMIT),
        cost_estimate=pl.CostEstimate(flops=8 * rows * part * part, bytes_accessed=18 * rows * part, transcendentals=0),
    )(place, attended, weight, *terms)


def split_kernel(at, marks, kept, got, send, keep):
    mine = marks[at + 1]
    for i in range(send.shape[0]):
        for out, side in ((send, 1 - mine), (keep, mine)):
            row = 2 * i + side
            out[i] = jnp.where(marks[at] > 0, kept[row].astype(jnp.float32), got[row].astype(jnp.float32)).astype(jnp.bfloat16)


def split(step, facts, kept, got):
    count, share, columns = kept.shape
    return pl.pallas_call(
        functools.partial(split_kernel, MARKS + 2 * step),
        out_shape=[jax.ShapeDtypeStruct((count // 2, share, columns), jnp.bfloat16)] * 2,
        in_specs=[smem(), vmem(), vmem()],
        out_specs=[vmem()] * 2,
        compiler_params=pltpu.CompilerParams(vmem_limit_bytes=SMALL_LIMIT),
        cost_estimate=pl.CostEstimate(flops=count * share * columns, bytes_accessed=6 * count * share * columns, transcendentals=0),
    )(facts, kept, got)


def turned(index):
    return index ^ (((index >> 3) & 1) << 2)


def head_kernel(marks, attended, latents, send, keep, scratch):
    part = attended.shape[1]
    tokf = scratch.shape[0]
    rows = pl.ds(pl.multiple_of(marks[HEAD] * tokf, tokf), tokf)
    scratch[:, :part] = attended[rows, :].astype(jnp.float32)
    scratch[:, part : 2 * part] = latents[rows, :].astype(jnp.float32)
    scratch[:, 2 * part :] = jnp.full((tokf, scratch.shape[1] - 2 * part), marks[HEAD + 2].astype(jnp.float32))
    share = send.shape[1]
    for i in range(send.shape[0]):
        for out, side in ((send, 1 - marks[HEAD + 1]), (keep, marks[HEAD + 1])):
            row = pl.multiple_of((turned(2 * i) + side) * share, share)
            out[i] = scratch[pl.ds(row, share), :].astype(jnp.bfloat16)


def share_kernel(place, kept, got, weight, rows, own, far):
    part = weight.shape[0]
    chosen = jnp.where(place[MARKS + 8] > 0, kept[0].astype(jnp.float32), got[0].astype(jnp.float32))
    rows[...] = chosen
    left = jnp.concatenate([chosen[:, :part]] * 2, axis=0).astype(jnp.bfloat16)
    for out, slots in ((own, (0, 2, 3, 4)), (far, (1, 5, 6, 7))):
        for i, slot in enumerate(slots):
            columns = pl.ds(pl.multiple_of(place[slot] * part, 128), part)
            result = jnp.dot(left, weight[:, columns], preferred_element_type=jnp.float32)
            out[i] = result[: out.shape[1]].astype(jnp.bfloat16)


def pass_kernel(own, far, *outs):
    for i, out in enumerate(outs):
        out[...] = added(own[i], far[i]).astype(jnp.bfloat16)


def estimate_kernel(rows, own, low, high, opposite, gates, out):
    part = own.shape[1]
    latent = rows[:, part : 2 * part]
    step = rows[0:1, 2 * part : 2 * part + 1]
    index = lax.broadcasted_iota(jnp.int32, gates.shape, 0).astype(jnp.float32) + 1.0
    gate = jnp.sum(jnp.where(index == step, gates[...].astype(jnp.float32), 0.0), axis=0, keepdims=True)
    velocity = (latent + gate * added(own[...], low[...], high[...], opposite[...])).astype(jnp.bfloat16)
    level = step / STEPS
    sigma = 3.0 * level / (1.0 + 2.0 * level)
    out[...] = (latent - sigma * velocity.astype(jnp.float32)).astype(jnp.bfloat16)


def velocity_kernel(facts, own, far, low, high, latents, gates, velocity):
    tokf = own.shape[0] // 2
    index = lax.broadcasted_iota(jnp.int32, gates.shape, 0) + 1
    for frame in range(2):
        at = slice(frame * tokf, (frame + 1) * tokf)
        gate = jnp.sum(jnp.where(index == facts[OWN_STEP + frame], gates[...].astype(jnp.float32), 0.0), axis=0, keepdims=True)
        projected = added(own[at, :], far[at, :], low[at, :], high[at, :])
        velocity[at, :] = (latents[at, :].astype(jnp.float32) + gate * projected).astype(jnp.bfloat16)


def small_call(kernel, in_specs, shapes, args, scratch=()):
    return pl.pallas_call(
        kernel,
        out_shape=shapes,
        in_specs=in_specs,
        out_specs=[vmem()] * len(shapes),
        scratch_shapes=list(scratch),
        compiler_params=pltpu.CompilerParams(vmem_limit_bytes=SMALL_LIMIT),
        cost_estimate=pl.CostEstimate(flops=1 << 20, bytes_accessed=1 << 20, transcendentals=0),
    )(*args)


def on_device(latents, step_index, head_index, band, mod_table, gate_table, qkv_weight, out_weight):
    rows, part = latents.shape
    frames = step_index.shape[0]
    tokf = rows // frames
    width = mod_table.shape[2]
    heads = band.shape[0]
    size = part // heads
    count = lax.axis_size("queue")
    me = lax.axis_index("queue")
    member = lax.axis_index("mp")
    frames_all = frames * count
    half = rows // 2
    x, y = member & 3, member >> 2
    slots = [yy * 4 + xx for yy, xx in (
        (y, x), (1 - y, x), (y, (x + 3) & 3), (y, (x + 1) & 3),
        (y, x ^ 2), (1 - y, (x + 3) & 3), (1 - y, (x + 1) & 3), (1 - y, x ^ 2),
    )]
    odd = me & 1 == 1
    head = head_index[0]
    position = (me * frames + jnp.arange(frames, dtype=jnp.int32) - head) & (frames_all - 1)
    offset = jnp.arange(5 * frames, dtype=jnp.int32)[None, :] - 2 * frames - jnp.arange(frames, dtype=jnp.int32)[:, None]
    other = position[:, None] + offset
    inside = (other >= 0) & (other < frames_all)
    near = jnp.abs(offset)[None, :, :] <= band[:, None, None]
    allowed = (inside[None, :, :] & near).reshape(-1)
    local_frame = head & 1
    mine, source = turned(me), turned(head >> 1)
    small = [jnp.where(odd, 1, 3), jnp.where(odd, 3, 1), local_frame, me & 1, lax.dynamic_index_in_dim(step_index, local_frame, 0, keepdims=False)]
    small += [step_index[f] for f in range(frames)]
    for bit in (1, 2, 4, 8, 16):
        small += [((source ^ mine) & bit) == 0, (mine & (2 * bit)) != 0]
    facts = jnp.concatenate([jnp.stack([jnp.asarray(v, jnp.int32) for v in slots]), allowed.astype(jnp.int32), jnp.stack([jnp.asarray(v, jnp.int32) for v in small])])

    cut = 96
    bf = jnp.bfloat16
    far, low, high = across(latents), ring(latents, 1), ring(latents, -1)
    far_opp = ring(far, 2)
    two_a = ring(jnp.concatenate([low[:half], far[:cut]]), 1)
    two_b = ring(jnp.concatenate([high[half:], far[rows - cut :]]), -1)
    two_c = across(jnp.concatenate([low[cut:], high[: rows - cut]]))

    modul = jnp.concatenate([lax.dynamic_index_in_dim(mod_table, step_index[f] - 1, 0) for f in range(frames)])
    kv, modulated = pl.pallas_call(
        qkv_kernel,
        out_shape=[jax.ShapeDtypeStruct((2, heads, rows, size), bf), jax.ShapeDtypeStruct((rows, width), bf)],
        in_specs=[smem(), anywhere()] + [vmem()] * 8 + [anywhere()],
        out_specs=[vmem()] * 2,
        scratch_shapes=[pltpu.VMEM((rows, part), bf), pltpu.VMEM((2, width, part), bf), pltpu.SemaphoreType.DMA((3,))],
        compiler_params=pltpu.CompilerParams(vmem_limit_bytes=VMEM_LIMIT),
        cost_estimate=pl.CostEstimate(flops=4 * rows * width * part, bytes_accessed=6 * width * part, transcendentals=0),
    )(facts, latents, far, low, high, far_opp, two_a, two_b, two_c, modul, qkv_weight)

    upper2 = shifted(kv, -2)
    lower2 = shifted(kv, 2)
    partner = flipped(kv, 1)
    query = pl.pallas_call(
        query_kernel,
        out_shape=jax.ShapeDtypeStruct((heads, rows, size), bf),
        in_specs=[anywhere()] * 2,
        out_specs=vmem(),
        scratch_shapes=[pltpu.VMEM((rows, width), bf), pltpu.VMEM((width, part), bf), pltpu.SemaphoreType.DMA((2,))],
        compiler_params=pltpu.CompilerParams(vmem_limit_bytes=VMEM_LIMIT),
        cost_estimate=pl.CostEstimate(flops=2 * rows * width * part, bytes_accessed=2 * width * part, transcendentals=0),
    )(modulated, qkv_weight)

    state = attend((2, 5), facts, query, (kv, partner))
    upper2, lower2, *state = lax.optimization_barrier((upper2, lower2, *state))
    passed = flipped(jnp.where(odd, lower2, upper2), 1)
    state = attend((4, 0), facts, query, (upper2, lower2), state)
    attended = attend((6,), facts, query, (passed,), state, last=True)

    sent_opp, two_a, two_b, two_c = summed(
        functools.partial(first_kernel, cut), facts, attended, out_weight, (), (rows, half + cut, half + cut, 2 * (rows - cut))
    )
    got = ring(sent_opp, 2), ring(two_a, -1), ring(two_b, 1), across(two_c)

    share = tokf // count
    wide = 2 * part + 128

    def shape(*dims, kind=bf):
        return jax.ShapeDtypeStruct(dims, kind)

    send, kept = small_call(
        head_kernel,
        [smem()] + [vmem()] * 2,
        [shape(count // 2, share, wide)] * 2,
        (facts, lax.optimization_barrier((attended, sent_opp))[0], latents),
        [pltpu.VMEM((tokf, wide), jnp.float32)],
    )
    moved = flipped(send, 1)
    for step in (0, 1, 2):
        send, kept = split(step, facts, kept, moved)
        moved = flipped(send, turned(2 << step))
    *got, moved = lax.optimization_barrier((*got, moved))
    sum_far, sum_low, sum_high, p_own = summed(functools.partial(second_kernel, cut), facts, attended, out_weight, got, (rows,) * 4)
    last = across(sum_far), ring(sum_low, -1), ring(sum_high, 1)
    send, kept = split(3, facts, kept, moved)
    moved = flipped(send, 16)
    held, mini_own, mini_far = small_call(
        share_kernel,
        [smem()] + [vmem()] * 3,
        [shape(share, wide, kind=jnp.float32)] + [shape(4, share, part)] * 2,
        (facts, kept, moved, out_weight),
    )
    *last, mini_far = lax.optimization_barrier((*last, across(mini_far)))
    own, low, high, opposite = small_call(pass_kernel, [vmem()] * 2, [shape(share, part)] * 4, (mini_own, mini_far))
    (head_frame,) = small_call(
        estimate_kernel,
        [vmem()] * 6,
        [shape(share, part)],
        (held, own, ring(low, -1), ring(high, 1), ring(opposite, 2), gate_table),
    )

    (velocity,) = small_call(
        velocity_kernel, [smem()] + [vmem()] * 6, [shape(rows, part)], (facts, p_own, *last, latents, gate_table)
    )
    return (velocity, head_frame)


def solution(mesh):
    placed = (
        P("queue", "mp"),
        P("queue"),
        P(),
        P("mp"),
        P(),
        P(None, "mp"),
        P(None, None, "mp"),
        P("mp", None),
    )
    return jax.shard_map(
        on_device,
        mesh=mesh,
        in_specs=placed,
        out_specs=(P("queue", "mp"), P("queue", "mp")),
        check_vma=False,
    )
```

```python
import functools

import jax
import jax.numpy as jnp
from jax import lax
from jax.experimental import pallas as pl
from jax.experimental.pallas import tpu as pltpu
from jax.sharding import PartitionSpec as P

STEPS = 50
EPS = 1e-06
BIG = 1e30
SEEN, WINDOW, HEAD, OWN_STEP, MARKS = 8, 68, 70, 73, 75
LOG2E = 1.4426950408889634
VMEM_LIMIT = 48 * 1024 * 1024
SMALL_LIMIT = 12 * 1024 * 1024


def ring(value, distance):
    return lax.ppermute(value, "mp", [(s, s // 4 * 4 + (s + distance) % 4) for s in range(8)])


def across(value):
    return lax.ppermute(value, "mp", [(s, s ^ 4) for s in range(8)])


def shifted(value, distance):
    count = lax.axis_size("queue")
    return lax.ppermute(value, "queue", [(s, (s + distance) % count) for s in range(count)])


def flipped(value, bit):
    return lax.ppermute(value, "queue", [(s, s ^ bit) for s in range(lax.axis_size("queue"))])


def vmem():
    return pl.BlockSpec(memory_space=pltpu.VMEM)


def anywhere():
    return pl.BlockSpec(memory_space=pl.ANY)


def smem():
    return pl.BlockSpec(memory_space=pltpu.SMEM)


def qkv_kernel(place, own_at, far, low, high, far_opp, two_a, two_b, two_c, modul, weight_at, kv, made, own, weight, sems):
    rows, part = own.shape
    half = rows // 2
    width = weight.shape[1]
    cut = two_a.shape[0] - half
    copies = [
        pltpu.make_async_copy(source, target, sems.at[i])
        for i, (source, target) in enumerate(((own_at, own), (weight_at.at[1], weight.at[0]), (weight_at.at[2], weight.at[1])))
    ]
    for copy in copies:
        copy.start()
    copies[0].wait()
    starts = [pl.multiple_of(place[i] * part, 128) for i in range(8)]
    chunk = 32
    for frame in range(2):
        for at in range(frame * half, (frame + 1) * half, chunk):
            parts = [
                (own, at), (far, at), (low, at), (high, at),
                (two_a, at) if at < half else (two_b, at - half),
                (two_a, half + at) if at < cut else (two_c, at - cut),
                (two_c, rows - cut + at) if at < rows - cut else (two_b, half + at - (rows - cut)),
                (far_opp, at),
            ]

            def load(i):
                ref, base = parts[i]
                return ref[base : base + chunk, :].astype(jnp.float32)

            total = load(0)
            for i in range(1, 8):
                total = total + load(i)
            mean = jnp.sum(total, axis=1, keepdims=True) * (1.0 / width)
            square = jnp.square(load(0) - mean)
            for i in range(1, 8):
                square = square + jnp.square(load(i) - mean)
            var = jnp.sum(square, axis=1, keepdims=True) * (1.0 / width)
            inverse = lax.rsqrt(var + EPS)
            for i in range(8):
                columns = pl.ds(starts[i], part)
                shift = modul[frame, 0:1, columns].astype(jnp.float32)
                scale = modul[frame, 1:2, columns].astype(jnp.float32) + 1.0
                value = (load(i) - mean) * inverse * scale + shift
                made[at : at + chunk, columns] = value.astype(jnp.bfloat16)
        left = made[frame * half : (frame + 1) * half, :]
        for which in range(2):
            if frame == 0:
                copies[1 + which].wait()
            result = jnp.dot(left, weight[which], preferred_element_type=jnp.float32).astype(jnp.bfloat16)
            for h in range(3):
                kv[which, h, frame * half : (frame + 1) * half, :] = result[:, h * 128 : (h + 1) * 128]


def query_kernel(made_at, weight_at, query, made, weight, sems):
    copies = [pltpu.make_async_copy(weight_at.at[0], weight, sems.at[0]), pltpu.make_async_copy(made_at, made, sems.at[1])]
    for copy in copies:
        copy.start()
    for copy in copies:
        copy.wait()
    result = jnp.dot(made[...], weight[...], preferred_element_type=jnp.float32).astype(jnp.bfloat16)
    for h in range(3):
        query[h] = result[:, h * 128 : (h + 1) * 128]


def attend_kernel(shape, allowed, query, *rest):
    blocks, first, last = shape
    keys, rest = rest[: len(blocks)], rest[len(blocks) :]
    if not first:
        top_in, sum_in, *rest = rest
    if last:
        out, scores = rest
    else:
        top_out, sum_out, scores = rest
    size = query.shape[2]
    tokf = query.shape[1] // 2
    factor = LOG2E / size**0.5
    ones = jnp.ones((tokf, size), jnp.bfloat16)
    for head, f in [(head, f) for head in range(query.shape[0]) for f in range(2)]:
        rows = slice(f * tokf, (f + 1) * tokf)
        q = query[head, rows, :]
        tiles = []
        for ref, slot in zip(keys, blocks):
            for g in range(2):
                if (slot, g, f) in ((0, 0, 1), (4, 1, 0)):
                    continue
                place = allowed[WINDOW + slot - 5] if slot >= 5 else slot
                tiles.append((ref, slice(g * tokf, (g + 1) * tokf), allowed[SEEN + (head * 2 + f) * 10 + place * 2 + g] > 0))
        top = jnp.full((tokf, size), -BIG, jnp.float32)
        for t, (ref, at, seen) in enumerate(tiles):
            s = lax.dot_general(q, ref[0, head, at, :], (((1,), (1,)), ((), ())), preferred_element_type=jnp.float32)
            scores[(head + f) % 2, t] = s
            top = jnp.maximum(top, jnp.where(seen, jnp.maximum(s[:, :size], s[:, size:]), -BIG))
        largest = jnp.broadcast_to(jnp.max(top, axis=1, keepdims=True) * factor, (tokf, size))
        total = jnp.zeros((tokf, 2 * size), jnp.float32)
        if not first:
            before = top_in[head, rows, :]
            largest = jnp.maximum(largest, before)
            fade = jnp.exp2(before - largest)
            total = sum_in[head, rows, :] * jnp.concatenate([fade, fade], axis=1)
        for t, (ref, at, seen) in enumerate(tiles):
            v = jnp.concatenate([ref[1, head, at, :], ones], axis=1)
            base = jnp.where(seen, largest, BIG)
            weights = jnp.concatenate(
                [jnp.exp2(scores[(head + f) % 2, t, :, i * size : (i + 1) * size] * factor - base) for i in range(2)], axis=1
            ).astype(jnp.bfloat16)
            total = total + jnp.dot(weights, v, preferred_element_type=jnp.float32)
        if last:
            out[rows, head * size : (head + 1) * size] = (total[:, :size] / total[:, size:]).astype(jnp.bfloat16)
        else:
            top_out[head, rows, :] = largest
            sum_out[head, rows, :] = total


def attend(blocks, allowed, query, keys, state=(), last=False):
    heads, rows, size = query.shape
    tokf = rows // 2
    if last:
        out_shape = jax.ShapeDtypeStruct((rows, heads * size), jnp.bfloat16)
    else:
        out_shape = [jax.ShapeDtypeStruct((heads, rows, n * size), jnp.float32) for n in (1, 2)]
    tiles = 4 * len(blocks)
    return pl.pallas_call(
        functools.partial(attend_kernel, (blocks, not state, last)),
        out_shape=out_shape,
        in_specs=[smem()] + [vmem()] * (1 + len(keys) + len(state)),
        out_specs=vmem() if last else [vmem()] * 2,
        scratch_shapes=[pltpu.VMEM((2, 2 * len(blocks), tokf, tokf), jnp.float32)],
        compiler_params=pltpu.CompilerParams(vmem_limit_bytes=SMALL_LIMIT),
        cost_estimate=pl.CostEstimate(
            flops=6 * heads * tiles * tokf * tokf * size, bytes_accessed=4 * tiles * tokf * size, transcendentals=heads * tiles * tokf * tokf
        ),
    )(allowed, query, *keys, *state)


def added(*terms):
    total = terms[0].astype(jnp.float32)
    for term in terms[1:]:
        total = total + term.astype(jnp.float32)
    return total


def product(place, slot, left, weight):
    part = weight.shape[0]
    columns = pl.ds(pl.multiple_of(place[slot] * part, 128), part)
    return jnp.dot(left, weight[:, columns], preferred_element_type=jnp.float32).astype(jnp.bfloat16)


def first_kernel(cut, place, attended, weight, far_opp, two_a, two_b, two_c):
    rows = attended.shape[0]
    half = rows // 2
    left = attended[...]
    far_opp[...] = product(place, 7, left, weight)
    opp, far_low, far_high = (product(place, slot, left, weight) for slot in (4, 5, 6))
    two_a[:half] = opp[:half]
    two_a[half:] = far_low[:cut]
    two_b[:half] = opp[half:]
    two_b[half:] = far_high[rows - cut :]
    two_c[: rows - cut] = far_low[cut:]
    two_c[rows - cut :] = far_high[: rows - cut]


def second_kernel(cut, place, attended, weight, got_opp, got_a, got_b, got_c, sum_far, sum_low, sum_high, own):
    rows = attended.shape[0]
    half = rows // 2
    bf = jnp.bfloat16
    left = attended[...]
    far, low, high = (product(place, slot, left, weight) for slot in (1, 2, 3))
    sum_far[:cut] = added(far[:cut], got_opp[:cut], got_a[half:]).astype(bf)
    sum_far[cut : rows - cut] = added(far[cut : rows - cut], got_opp[cut : rows - cut]).astype(bf)
    sum_far[rows - cut :] = added(far[rows - cut :], got_opp[rows - cut :], got_b[half:]).astype(bf)
    sum_low[:cut] = added(low[:cut], got_a[:cut]).astype(bf)
    sum_low[cut:half] = added(low[cut:half], got_a[cut:half], got_c[: half - cut]).astype(bf)
    sum_low[half:] = added(low[half:], got_c[half - cut : rows - cut]).astype(bf)
    sum_high[:half] = added(high[:half], got_c[rows - cut : rows - cut + half]).astype(bf)
    sum_high[half : rows - cut] = added(high[half : rows - cut], got_b[: half - cut], got_c[rows - cut + half :]).astype(bf)
    sum_high[rows - cut :] = added(high[rows - cut :], got_b[half - cut : half]).astype(bf)
    own[...] = product(place, 0, left, weight)


def summed(kernel, place, attended, weight, terms, heights):
    rows, part = attended.shape
    return pl.pallas_call(
        kernel,
        out_shape=[jax.ShapeDtypeStruct((height, part), jnp.bfloat16) for height in heights],
        in_specs=[smem()] + [vmem()] * (2 + len(terms)),
        out_specs=[vmem()] * len(heights),
        compiler_params=pltpu.CompilerParams(vmem_limit_bytes=SMALL_LIMIT),
        cost_estimate=pl.CostEstimate(flops=8 * rows * part * part, bytes_accessed=18 * rows * part, transcendentals=0),
    )(place, attended, weight, *terms)


def split_kernel(at, marks, kept, got, send, keep):
    mine = marks[at + 1]
    for i in range(send.shape[0]):
        for out, side in ((send, 1 - mine), (keep, mine)):
            row = 2 * i + side
            out[i] = jnp.where(marks[at] > 0, kept[row].astype(jnp.float32), got[row].astype(jnp.float32)).astype(jnp.bfloat16)


def split(step, facts, kept, got):
    count, share, columns = kept.shape
    return pl.pallas_call(
        functools.partial(split_kernel, MARKS + 2 * step),
        out_shape=[jax.ShapeDtypeStruct((count // 2, share, columns), jnp.bfloat16)] * 2,
        in_specs=[smem(), vmem(), vmem()],
        out_specs=[vmem()] * 2,
        compiler_params=pltpu.CompilerParams(vmem_limit_bytes=SMALL_LIMIT),
        cost_estimate=pl.CostEstimate(flops=count * share * columns, bytes_accessed=6 * count * share * columns, transcendentals=0),
    )(facts, kept, got)


def turned(index):
    return index ^ (((index >> 3) & 1) << 2)


def head_kernel(marks, attended, latents, send, keep, scratch):
    part = attended.shape[1]
    tokf = scratch.shape[0]
    rows = pl.ds(pl.multiple_of(marks[HEAD] * tokf, tokf), tokf)
    scratch[:, :part] = attended[rows, :].astype(jnp.float32)
    scratch[:, part : 2 * part] = latents[rows, :].astype(jnp.float32)
    scratch[:, 2 * part :] = jnp.full((tokf, scratch.shape[1] - 2 * part), marks[HEAD + 2].astype(jnp.float32))
    share = send.shape[1]
    for i in range(send.shape[0]):
        for out, side in ((send, 1 - marks[HEAD + 1]), (keep, marks[HEAD + 1])):
            row = pl.multiple_of((turned(2 * i) + side) * share, share)
            out[i] = scratch[pl.ds(row, share), :].astype(jnp.bfloat16)


def share_kernel(place, kept, got, weight, rows, own, far):
    part = weight.shape[0]
    chosen = jnp.where(place[MARKS + 8] > 0, kept[0].astype(jnp.float32), got[0].astype(jnp.float32))
    rows[...] = chosen
    left = jnp.concatenate([chosen[:, :part]] * 2, axis=0).astype(jnp.bfloat16)
    for out, slots in ((own, (0, 2, 3, 4)), (far, (1, 5, 6, 7))):
        for i, slot in enumerate(slots):
            columns = pl.ds(pl.multiple_of(place[slot] * part, 128), part)
            result = jnp.dot(left, weight[:, columns], preferred_element_type=jnp.float32)
            out[i] = result[: out.shape[1]].astype(jnp.bfloat16)


def pass_kernel(own, far, *outs):
    for i, out in enumerate(outs):
        out[...] = added(own[i], far[i]).astype(jnp.bfloat16)


def estimate_kernel(rows, own, low, high, opposite, gates, out):
    part = own.shape[1]
    latent = rows[:, part : 2 * part]
    step = rows[0:1, 2 * part : 2 * part + 1]
    index = lax.broadcasted_iota(jnp.int32, gates.shape, 0).astype(jnp.float32) + 1.0
    gate = jnp.sum(jnp.where(index == step, gates[...].astype(jnp.float32), 0.0), axis=0, keepdims=True)
    velocity = (latent + gate * added(own[...], low[...], high[...], opposite[...])).astype(jnp.bfloat16)
    level = step / STEPS
    sigma = 3.0 * level / (1.0 + 2.0 * level)
    out[...] = (latent - sigma * velocity.astype(jnp.float32)).astype(jnp.bfloat16)


def velocity_kernel(facts, own, far, low, high, latents, gates, velocity):
    tokf = own.shape[0] // 2
    index = lax.broadcasted_iota(jnp.int32, gates.shape, 0) + 1
    for frame in range(2):
        at = slice(frame * tokf, (frame + 1) * tokf)
        gate = jnp.sum(jnp.where(index == facts[OWN_STEP + frame], gates[...].astype(jnp.float32), 0.0), axis=0, keepdims=True)
        projected = added(own[at, :], far[at, :], low[at, :], high[at, :])
        velocity[at, :] = (latents[at, :].astype(jnp.float32) + gate * projected).astype(jnp.bfloat16)


def small_call(kernel, in_specs, shapes, args, scratch=()):
    return pl.pallas_call(
        kernel,
        out_shape=shapes,
        in_specs=in_specs,
        out_specs=[vmem()] * len(shapes),
        scratch_shapes=list(scratch),
        compiler_params=pltpu.CompilerParams(vmem_limit_bytes=SMALL_LIMIT),
        cost_estimate=pl.CostEstimate(flops=1 << 20, bytes_accessed=1 << 20, transcendentals=0),
    )(*args)


def on_device(latents, step_index, head_index, band, mod_table, gate_table, qkv_weight, out_weight):
    rows, part = latents.shape
    frames = step_index.shape[0]
    tokf = rows // frames
    width = mod_table.shape[2]
    heads = band.shape[0]
    size = part // heads
    count = lax.axis_size("queue")
    me = lax.axis_index("queue")
    member = lax.axis_index("mp")
    frames_all = frames * count
    half = rows // 2
    x, y = member & 3, member >> 2
    slots = [yy * 4 + xx for yy, xx in (
        (y, x), (1 - y, x), (y, (x + 3) & 3), (y, (x + 1) & 3),
        (y, x ^ 2), (1 - y, (x + 3) & 3), (1 - y, (x + 1) & 3), (1 - y, x ^ 2),
    )]
    odd = me & 1 == 1
    head = head_index[0]
    position = (me * frames + jnp.arange(frames, dtype=jnp.int32) - head) & (frames_all - 1)
    offset = jnp.arange(5 * frames, dtype=jnp.int32)[None, :] - 2 * frames - jnp.arange(frames, dtype=jnp.int32)[:, None]
    other = position[:, None] + offset
    inside = (other >= 0) & (other < frames_all)
    near = jnp.abs(offset)[None, :, :] <= band[:, None, None]
    allowed = (inside[None, :, :] & near).reshape(-1)
    local_frame = head & 1
    mine, source = turned(me), turned(head >> 1)
    small = [jnp.where(odd, 1, 3), jnp.where(odd, 3, 1), local_frame, me & 1, lax.dynamic_index_in_dim(step_index, local_frame, 0, keepdims=False)]
    small += [step_index[f] for f in range(frames)]
    for bit in (1, 2, 4, 8, 16):
        small += [((source ^ mine) & bit) == 0, (mine & (2 * bit)) != 0]
    facts = jnp.concatenate([jnp.stack([jnp.asarray(v, jnp.int32) for v in slots]), allowed.astype(jnp.int32), jnp.stack([jnp.asarray(v, jnp.int32) for v in small])])

    cut = 64
    bf = jnp.bfloat16
    far, low, high = across(latents), ring(latents, 1), ring(latents, -1)
    far_opp = ring(far, 2)
    two_a = ring(jnp.concatenate([low[:half], far[:cut]]), 1)
    two_b = ring(jnp.concatenate([high[half:], far[rows - cut :]]), -1)
    two_c = across(jnp.concatenate([low[cut:], high[: rows - cut]]))

    modul = jnp.concatenate([lax.dynamic_index_in_dim(mod_table, step_index[f] - 1, 0) for f in range(frames)])
    kv, modulated = pl.pallas_call(
        qkv_kernel,
        out_shape=[jax.ShapeDtypeStruct((2, heads, rows, size), bf), jax.ShapeDtypeStruct((rows, width), bf)],
        in_specs=[smem(), anywhere()] + [vmem()] * 8 + [anywhere()],
        out_specs=[vmem()] * 2,
        scratch_shapes=[pltpu.VMEM((rows, part), bf), pltpu.VMEM((2, width, part), bf), pltpu.SemaphoreType.DMA((3,))],
        compiler_params=pltpu.CompilerParams(vmem_limit_bytes=VMEM_LIMIT),
        cost_estimate=pl.CostEstimate(flops=4 * rows * width * part, bytes_accessed=6 * width * part, transcendentals=0),
    )(facts, latents, far, low, high, far_opp, two_a, two_b, two_c, modul, qkv_weight)

    upper2 = shifted(kv, -2)
    lower2 = shifted(kv, 2)
    partner = flipped(kv, 1)
    query = pl.pallas_call(
        query_kernel,
        out_shape=jax.ShapeDtypeStruct((heads, rows, size), bf),
        in_specs=[anywhere()] * 2,
        out_specs=vmem(),
        scratch_shapes=[pltpu.VMEM((rows, width), bf), pltpu.VMEM((width, part), bf), pltpu.SemaphoreType.DMA((2,))],
        compiler_params=pltpu.CompilerParams(vmem_limit_bytes=VMEM_LIMIT),
        cost_estimate=pl.CostEstimate(flops=2 * rows * width * part, bytes_accessed=2 * width * part, transcendentals=0),
    )(modulated, qkv_weight)

    state = attend((2, 5), facts, query, (kv, partner))
    upper2, lower2, *state = lax.optimization_barrier((upper2, lower2, *state))
    passed = flipped(jnp.where(odd, lower2, upper2), 1)
    state = attend((4, 0), facts, query, (upper2, lower2), state)
    attended = attend((6,), facts, query, (passed,), state, last=True)

    sent_opp, two_a, two_b, two_c = summed(
        functools.partial(first_kernel, cut), facts, attended, out_weight, (), (rows, half + cut, half + cut, 2 * (rows - cut))
    )
    got = ring(sent_opp, 2), ring(two_a, -1), ring(two_b, 1), across(two_c)

    share = tokf // count
    wide = 2 * part + 128

    def shape(*dims, kind=bf):
        return jax.ShapeDtypeStruct(dims, kind)

    send, kept = small_call(
        head_kernel,
        [smem()] + [vmem()] * 2,
        [shape(count // 2, share, wide)] * 2,
        (facts, lax.optimization_barrier((attended, sent_opp))[0], latents),
        [pltpu.VMEM((tokf, wide), jnp.float32)],
    )
    moved = flipped(send, 1)
    for step in (0, 1, 2):
        send, kept = split(step, facts, kept, moved)
        moved = flipped(send, turned(2 << step))
    *got, moved = lax.optimization_barrier((*got, moved))
    sum_far, sum_low, sum_high, p_own = summed(functools.partial(second_kernel, cut), facts, attended, out_weight, got, (rows,) * 4)
    last = across(sum_far), ring(sum_low, -1), ring(sum_high, 1)
    send, kept = split(3, facts, kept, moved)
    moved = flipped(send, 16)
    held, mini_own, mini_far = small_call(
        share_kernel,
        [smem()] + [vmem()] * 3,
        [shape(share, wide, kind=jnp.float32)] + [shape(4, share, part)] * 2,
        (facts, kept, moved, out_weight),
    )
    *last, mini_far = lax.optimization_barrier((*last, across(mini_far)))
    own, low, high, opposite = small_call(pass_kernel, [vmem()] * 2, [shape(share, part)] * 4, (mini_own, mini_far))
    (head_frame,) = small_call(
        estimate_kernel,
        [vmem()] * 6,
        [shape(share, part)],
        (held, own, ring(low, -1), ring(high, 1), ring(opposite, 2), gate_table),
    )

    (velocity,) = small_call(
        velocity_kernel, [smem()] + [vmem()] * 6, [shape(rows, part)], (facts, p_own, *last, latents, gate_table)
    )
    return (velocity, head_frame)


def solution(mesh):
    placed = (
        P("queue", "mp"),
        P("queue"),
        P(),
        P("mp"),
        P(),
        P(None, "mp"),
        P(None, None, "mp"),
        P("mp", None),
    )
    return jax.shard_map(
        on_device,
        mesh=mesh,
        in_specs=placed,
        out_specs=(P("queue", "mp"), P("queue", "mp")),
        check_vma=False,
    )
```

```python
import functools

import jax
import jax.numpy as jnp
from jax import lax
from jax.experimental import pallas as pl
from jax.experimental.pallas import tpu as pltpu
from jax.sharding import PartitionSpec as P

STEPS = 50
EPS = 1e-06
BIG = 1e30
SEEN, WINDOW, HEAD, OWN_STEP, MARKS = 8, 68, 70, 73, 75
LOG2E = 1.4426950408889634
VMEM_LIMIT = 48 * 1024 * 1024
SMALL_LIMIT = 12 * 1024 * 1024


def ring(value, distance):
    return lax.ppermute(value, "mp", [(s, s // 4 * 4 + (s + distance) % 4) for s in range(8)])


def across(value):
    return lax.ppermute(value, "mp", [(s, s ^ 4) for s in range(8)])


def shifted(value, distance):
    count = lax.axis_size("queue")
    return lax.ppermute(value, "queue", [(s, (s + distance) % count) for s in range(count)])


def flipped(value, bit):
    return lax.ppermute(value, "queue", [(s, s ^ bit) for s in range(lax.axis_size("queue"))])


def vmem():
    return pl.BlockSpec(memory_space=pltpu.VMEM)


def anywhere():
    return pl.BlockSpec(memory_space=pl.ANY)


def smem():
    return pl.BlockSpec(memory_space=pltpu.SMEM)


def product_kernel(first, place, own_at, far, low, high, far_opp, two_a, two_b, two_c, modul, weight_at, out, made, own, weight, sems):
    rows, part = own.shape
    half = rows // 2
    width = weight.shape[0]
    cut = two_a.shape[0] - half
    copies = [
        pltpu.make_async_copy(source, target, sems.at[i])
        for i, (source, target) in enumerate(((own_at, own), *((weight_at.at[first + which], weight.at[:, which * part : (which + 1) * part]) for which in range(out.shape[0]))))
    ]
    for copy in copies:
        copy.start()
    copies[0].wait()
    starts = [pl.multiple_of(place[i] * part, 128) for i in range(8)]
    chunk = 32
    for frame in range(2):
        for at in range(frame * half, (frame + 1) * half, chunk):
            parts = [
                (own, at), (far, at), (low, at), (high, at),
                (two_a, at) if at < half else (two_b, at - half),
                (two_a, half + at) if at < cut else (two_c, at - cut),
                (two_c, rows - cut + at) if at < rows - cut else (two_b, half + at - (rows - cut)),
                (far_opp, at),
            ]

            def load(i):
                ref, base = parts[i]
                return ref[base : base + chunk, :].astype(jnp.float32)

            total = load(0)
            for i in range(1, 8):
                total = total + load(i)
            mean = jnp.sum(total, axis=1, keepdims=True) * (1.0 / width)
            square = jnp.square(load(0) - mean)
            for i in range(1, 8):
                square = square + jnp.square(load(i) - mean)
            var = jnp.sum(square, axis=1, keepdims=True) * (1.0 / width)
            inverse = lax.rsqrt(var + EPS)
            for i in range(8):
                columns = pl.ds(starts[i], part)
                shift = modul[frame, 0:1, columns].astype(jnp.float32)
                scale = modul[frame, 1:2, columns].astype(jnp.float32) + 1.0
                value = (load(i) - mean) * inverse * scale + shift
                made[at : at + chunk, columns] = value.astype(jnp.bfloat16)
    for copy in copies[1:]:
        copy.wait()
    result = jnp.dot(made[...], weight[...], preferred_element_type=jnp.float32).astype(jnp.bfloat16)
    for which in range(out.shape[0]):
        for h in range(3):
            at = which * part + h * 128
            out[which, h] = result[:, at : at + 128]


def products(first, count, heads, facts, latents, blocks, modul, weight):
    rows, part = latents.shape
    width = weight.shape[1]
    bf = jnp.bfloat16
    return pl.pallas_call(
        functools.partial(product_kernel, first),
        out_shape=jax.ShapeDtypeStruct((count, heads, rows, part // heads), bf),
        in_specs=[smem(), anywhere()] + [vmem()] * 8 + [anywhere()],
        out_specs=vmem(),
        scratch_shapes=[
            pltpu.VMEM((rows, width), bf),
            pltpu.VMEM((rows, part), bf),
            pltpu.VMEM((width, count * part), bf),
            pltpu.SemaphoreType.DMA((1 + count,)),
        ],
        compiler_params=pltpu.CompilerParams(vmem_limit_bytes=VMEM_LIMIT),
        cost_estimate=pl.CostEstimate(flops=2 * count * rows * width * part, bytes_accessed=2 * (count + 1) * width * part, transcendentals=0),
    )(facts, latents, *blocks, modul, weight)


def attend_kernel(shape, allowed, query, *rest):
    blocks, first, last = shape
    keys, rest = rest[: len(blocks)], rest[len(blocks) :]
    if not first:
        top_in, sum_in, *rest = rest
    if last:
        out, scores = rest
    else:
        top_out, sum_out, scores = rest
    size = query.shape[2]
    tokf = query.shape[1] // 2
    factor = LOG2E / size**0.5
    ones = jnp.ones((tokf, size), jnp.bfloat16)
    for head, f in [(head, f) for head in range(query.shape[0]) for f in range(2)]:
        rows = slice(f * tokf, (f + 1) * tokf)
        q = query[head, rows, :]
        tiles = []
        for ref, slot in zip(keys, blocks):
            for g in range(2):
                if (slot, g, f) in ((0, 0, 1), (4, 1, 0)):
                    continue
                place = allowed[WINDOW + slot - 5] if slot >= 5 else slot
                tiles.append((ref, slice(g * tokf, (g + 1) * tokf), allowed[SEEN + (head * 2 + f) * 10 + place * 2 + g] > 0))
        top = jnp.full((tokf, size), -BIG, jnp.float32)
        for t, (ref, at, seen) in enumerate(tiles):
            s = lax.dot_general(q, ref[0, head, at, :], (((1,), (1,)), ((), ())), preferred_element_type=jnp.float32)
            scores[(head + f) % 2, t] = s
            top = jnp.maximum(top, jnp.where(seen, jnp.maximum(s[:, :size], s[:, size:]), -BIG))
        largest = jnp.broadcast_to(jnp.max(top, axis=1, keepdims=True) * factor, (tokf, size))
        total = jnp.zeros((tokf, 2 * size), jnp.float32)
        if not first:
            before = top_in[head, rows, :]
            largest = jnp.maximum(largest, before)
            fade = jnp.exp2(before - largest)
            total = sum_in[head, rows, :] * jnp.concatenate([fade, fade], axis=1)
        for t, (ref, at, seen) in enumerate(tiles):
            v = jnp.concatenate([ref[1, head, at, :], ones], axis=1)
            base = jnp.where(seen, largest, BIG)
            weights = jnp.concatenate(
                [jnp.exp2(scores[(head + f) % 2, t, :, i * size : (i + 1) * size] * factor - base) for i in range(2)], axis=1
            ).astype(jnp.bfloat16)
            total = total + jnp.dot(weights, v, preferred_element_type=jnp.float32)
        if last:
            out[rows, head * size : (head + 1) * size] = (total[:, :size] / total[:, size:]).astype(jnp.bfloat16)
        else:
            top_out[head, rows, :] = largest
            sum_out[head, rows, :] = total


def attend(blocks, allowed, query, keys, state=(), last=False):
    heads, rows, size = query.shape
    tokf = rows // 2
    if last:
        out_shape = jax.ShapeDtypeStruct((rows, heads * size), jnp.bfloat16)
    else:
        out_shape = [jax.ShapeDtypeStruct((heads, rows, n * size), jnp.float32) for n in (1, 2)]
    tiles = 4 * len(blocks)
    return pl.pallas_call(
        functools.partial(attend_kernel, (blocks, not state, last)),
        out_shape=out_shape,
        in_specs=[smem()] + [vmem()] * (1 + len(keys) + len(state)),
        out_specs=vmem() if last else [vmem()] * 2,
        scratch_shapes=[pltpu.VMEM((2, 2 * len(blocks), tokf, tokf), jnp.float32)],
        compiler_params=pltpu.CompilerParams(vmem_limit_bytes=SMALL_LIMIT),
        cost_estimate=pl.CostEstimate(
            flops=6 * heads * tiles * tokf * tokf * size, bytes_accessed=4 * tiles * tokf * size, transcendentals=heads * tiles * tokf * tokf
        ),
    )(allowed, query, *keys, *state)


def added(*terms):
    total = terms[0].astype(jnp.float32)
    for term in terms[1:]:
        total = total + term.astype(jnp.float32)
    return total


def product(place, slot, left, weight):
    part = weight.shape[0]
    columns = pl.ds(pl.multiple_of(place[slot] * part, 128), part)
    return jnp.dot(left, weight[:, columns], preferred_element_type=jnp.float32).astype(jnp.bfloat16)


def first_kernel(cut, place, attended, weight, far_opp, two_a, two_b, two_c):
    rows = attended.shape[0]
    half = rows // 2
    left = attended[...]
    far_opp[...] = product(place, 7, left, weight)
    opp, far_low, far_high = (product(place, slot, left, weight) for slot in (4, 5, 6))
    two_a[:half] = opp[:half]
    two_a[half:] = far_low[:cut]
    two_b[:half] = opp[half:]
    two_b[half:] = far_high[rows - cut :]
    two_c[: rows - cut] = far_low[cut:]
    two_c[rows - cut :] = far_high[: rows - cut]


def second_kernel(cut, place, attended, weight, got_opp, got_a, got_b, got_c, sum_far, sum_low, sum_high, own):
    rows = attended.shape[0]
    half = rows // 2
    bf = jnp.bfloat16
    left = attended[...]
    far, low, high = (product(place, slot, left, weight) for slot in (1, 2, 3))
    sum_far[:cut] = added(far[:cut], got_opp[:cut], got_a[half:]).astype(bf)
    sum_far[cut : rows - cut] = added(far[cut : rows - cut], got_opp[cut : rows - cut]).astype(bf)
    sum_far[rows - cut :] = added(far[rows - cut :], got_opp[rows - cut :], got_b[half:]).astype(bf)
    sum_low[:cut] = added(low[:cut], got_a[:cut]).astype(bf)
    sum_low[cut:half] = added(low[cut:half], got_a[cut:half], got_c[: half - cut]).astype(bf)
    sum_low[half:] = added(low[half:], got_c[half - cut : rows - cut]).astype(bf)
    sum_high[:half] = added(high[:half], got_c[rows - cut : rows - cut + half]).astype(bf)
    sum_high[half : rows - cut] = added(high[half : rows - cut], got_b[: half - cut], got_c[rows - cut + half :]).astype(bf)
    sum_high[rows - cut :] = added(high[rows - cut :], got_b[half - cut : half]).astype(bf)
    own[...] = product(place, 0, left, weight)


def summed(kernel, place, attended, weight, terms, heights):
    rows, part = attended.shape
    return pl.pallas_call(
        kernel,
        out_shape=[jax.ShapeDtypeStruct((height, part), jnp.bfloat16) for height in heights],
        in_specs=[smem()] + [vmem()] * (2 + len(terms)),
        out_specs=[vmem()] * len(heights),
        compiler_params=pltpu.CompilerParams(vmem_limit_bytes=SMALL_LIMIT),
        cost_estimate=pl.CostEstimate(flops=8 * rows * part * part, bytes_accessed=18 * rows * part, transcendentals=0),
    )(place, attended, weight, *terms)


def split_kernel(at, marks, kept, got, send, keep):
    mine = marks[at + 1]
    for i in range(send.shape[0]):
        for out, side in ((send, 1 - mine), (keep, mine)):
            row = 2 * i + side
            out[i] = jnp.where(marks[at] > 0, kept[row].astype(jnp.float32), got[row].astype(jnp.float32)).astype(jnp.bfloat16)


def split(step, facts, kept, got):
    count, share, columns = kept.shape
    return pl.pallas_call(
        functools.partial(split_kernel, MARKS + 2 * step),
        out_shape=[jax.ShapeDtypeStruct((count // 2, share, columns), jnp.bfloat16)] * 2,
        in_specs=[smem(), vmem(), vmem()],
        out_specs=[vmem()] * 2,
        compiler_params=pltpu.CompilerParams(vmem_limit_bytes=SMALL_LIMIT),
        cost_estimate=pl.CostEstimate(flops=count * share * columns, bytes_accessed=6 * count * share * columns, transcendentals=0),
    )(facts, kept, got)


def turned(index):
    return index ^ (((index >> 3) & 1) << 2)


def head_kernel(marks, attended, latents, send, keep, scratch):
    part = attended.shape[1]
    tokf = scratch.shape[0]
    rows = pl.ds(pl.multiple_of(marks[HEAD] * tokf, tokf), tokf)
    scratch[:, :part] = attended[rows, :].astype(jnp.float32)
    scratch[:, part : 2 * part] = latents[rows, :].astype(jnp.float32)
    scratch[:, 2 * part :] = jnp.full((tokf, scratch.shape[1] - 2 * part), marks[HEAD + 2].astype(jnp.float32))
    share = send.shape[1]
    for i in range(send.shape[0]):
        for out, side in ((send, 1 - marks[HEAD + 1]), (keep, marks[HEAD + 1])):
            row = pl.multiple_of((turned(2 * i) + side) * share, share)
            out[i] = scratch[pl.ds(row, share), :].astype(jnp.bfloat16)


def share_kernel(place, kept, got, weight, rows, own, far):
    part = weight.shape[0]
    chosen = jnp.where(place[MARKS + 8] > 0, kept[0].astype(jnp.float32), got[0].astype(jnp.float32))
    rows[...] = chosen
    left = jnp.concatenate([chosen[:, :part]] * 2, axis=0).astype(jnp.bfloat16)
    for out, slots in ((own, (0, 2, 3, 4)), (far, (1, 5, 6, 7))):
        for i, slot in enumerate(slots):
            columns = pl.ds(pl.multiple_of(place[slot] * part, 128), part)
            result = jnp.dot(left, weight[:, columns], preferred_element_type=jnp.float32)
            out[i] = result[: out.shape[1]].astype(jnp.bfloat16)


def pass_kernel(own, far, *outs):
    for i, out in enumerate(outs):
        out[...] = added(own[i], far[i]).astype(jnp.bfloat16)


def estimate_kernel(rows, own, low, high, opposite, gates, out):
    part = own.shape[1]
    latent = rows[:, part : 2 * part]
    step = rows[0:1, 2 * part : 2 * part + 1]
    index = lax.broadcasted_iota(jnp.int32, gates.shape, 0).astype(jnp.float32) + 1.0
    gate = jnp.sum(jnp.where(index == step, gates[...].astype(jnp.float32), 0.0), axis=0, keepdims=True)
    velocity = (latent + gate * added(own[...], low[...], high[...], opposite[...])).astype(jnp.bfloat16)
    level = step / STEPS
    sigma = 3.0 * level / (1.0 + 2.0 * level)
    out[...] = (latent - sigma * velocity.astype(jnp.float32)).astype(jnp.bfloat16)


def velocity_kernel(facts, own, far, low, high, latents, gates, velocity):
    tokf = own.shape[0] // 2
    index = lax.broadcasted_iota(jnp.int32, gates.shape, 0) + 1
    for frame in range(2):
        at = slice(frame * tokf, (frame + 1) * tokf)
        gate = jnp.sum(jnp.where(index == facts[OWN_STEP + frame], gates[...].astype(jnp.float32), 0.0), axis=0, keepdims=True)
        projected = added(own[at, :], far[at, :], low[at, :], high[at, :])
        velocity[at, :] = (latents[at, :].astype(jnp.float32) + gate * projected).astype(jnp.bfloat16)


def small_call(kernel, in_specs, shapes, args, scratch=()):
    return pl.pallas_call(
        kernel,
        out_shape=shapes,
        in_specs=in_specs,
        out_specs=[vmem()] * len(shapes),
        scratch_shapes=list(scratch),
        compiler_params=pltpu.CompilerParams(vmem_limit_bytes=SMALL_LIMIT),
        cost_estimate=pl.CostEstimate(flops=1 << 20, bytes_accessed=1 << 20, transcendentals=0),
    )(*args)


def on_device(latents, step_index, head_index, band, mod_table, gate_table, qkv_weight, out_weight):
    rows, part = latents.shape
    frames = step_index.shape[0]
    tokf = rows // frames
    width = mod_table.shape[2]
    heads = band.shape[0]
    size = part // heads
    count = lax.axis_size("queue")
    me = lax.axis_index("queue")
    member = lax.axis_index("mp")
    frames_all = frames * count
    half = rows // 2
    x, y = member & 3, member >> 2
    slots = [yy * 4 + xx for yy, xx in (
        (y, x), (1 - y, x), (y, (x + 3) & 3), (y, (x + 1) & 3),
        (y, x ^ 2), (1 - y, (x + 3) & 3), (1 - y, (x + 1) & 3), (1 - y, x ^ 2),
    )]
    odd = me & 1 == 1
    head = head_index[0]
    position = (me * frames + jnp.arange(frames, dtype=jnp.int32) - head) & (frames_all - 1)
    offset = jnp.arange(5 * frames, dtype=jnp.int32)[None, :] - 2 * frames - jnp.arange(frames, dtype=jnp.int32)[:, None]
    other = position[:, None] + offset
    inside = (other >= 0) & (other < frames_all)
    near = jnp.abs(offset)[None, :, :] <= band[:, None, None]
    allowed = (inside[None, :, :] & near).reshape(-1)
    local_frame = head & 1
    mine, source = turned(me), turned(head >> 1)
    small = [jnp.where(odd, 1, 3), jnp.where(odd, 3, 1), local_frame, me & 1, lax.dynamic_index_in_dim(step_index, local_frame, 0, keepdims=False)]
    small += [step_index[f] for f in range(frames)]
    for bit in (1, 2, 4, 8, 16):
        small += [((source ^ mine) & bit) == 0, (mine & (2 * bit)) != 0]
    facts = jnp.concatenate([jnp.stack([jnp.asarray(v, jnp.int32) for v in slots]), allowed.astype(jnp.int32), jnp.stack([jnp.asarray(v, jnp.int32) for v in small])])

    cut = 64
    bf = jnp.bfloat16
    far, low, high = across(latents), ring(latents, 1), ring(latents, -1)
    far_opp = ring(far, 2)
    two_a = ring(jnp.concatenate([low[:half], far[:cut]]), 1)
    two_b = ring(jnp.concatenate([high[half:], far[rows - cut :]]), -1)
    two_c = across(jnp.concatenate([low[cut:], high[: rows - cut]]))

    modul = jnp.concatenate([lax.dynamic_index_in_dim(mod_table, step_index[f] - 1, 0) for f in range(frames)])
    blocks = (far, low, high, far_opp, two_a, two_b, two_c)
    kv = products(1, 2, heads, facts, latents, blocks, modul, qkv_weight)

    upper2 = shifted(kv, -2)
    lower2 = shifted(kv, 2)
    partner = flipped(kv, 1)
    query = products(0, 1, heads, facts, latents, blocks, modul, qkv_weight)[0]

    state = attend((2, 5), facts, query, (kv, partner))
    upper2, lower2, *state = lax.optimization_barrier((upper2, lower2, *state))
    passed = flipped(jnp.where(odd, lower2, upper2), 1)
    state = attend((4, 0), facts, query, (upper2, lower2), state)
    attended = attend((6,), facts, query, (passed,), state, last=True)

    sent_opp, two_a, two_b, two_c = summed(
        functools.partial(first_kernel, cut), facts, attended, out_weight, (), (rows, half + cut, half + cut, 2 * (rows - cut))
    )
    got = ring(sent_opp, 2), ring(two_a, -1), ring(two_b, 1), across(two_c)

    share = tokf // count
    wide = 2 * part + 128

    def shape(*dims, kind=bf):
        return jax.ShapeDtypeStruct(dims, kind)

    send, kept = small_call(
        head_kernel,
        [smem()] + [vmem()] * 2,
        [shape(count // 2, share, wide)] * 2,
        (facts, lax.optimization_barrier((attended, sent_opp))[0], latents),
        [pltpu.VMEM((tokf, wide), jnp.float32)],
    )
    moved = flipped(send, 1)
    for step in (0, 1, 2):
        send, kept = split(step, facts, kept, moved)
        moved = flipped(send, turned(2 << step))
    *got, moved = lax.optimization_barrier((*got, moved))
    sum_far, sum_low, sum_high, p_own = summed(functools.partial(second_kernel, cut), facts, attended, out_weight, got, (rows,) * 4)
    last = across(sum_far), ring(sum_low, -1), ring(sum_high, 1)
    send, kept = split(3, facts, kept, moved)
    moved = flipped(send, 16)
    held, mini_own, mini_far = small_call(
        share_kernel,
        [smem()] + [vmem()] * 3,
        [shape(share, wide, kind=jnp.float32)] + [shape(4, share, part)] * 2,
        (facts, kept, moved, out_weight),
    )
    *last, mini_far = lax.optimization_barrier((*last, across(mini_far)))
    own, low, high, opposite = small_call(pass_kernel, [vmem()] * 2, [shape(share, part)] * 4, (mini_own, mini_far))
    (head_frame,) = small_call(
        estimate_kernel,
        [vmem()] * 6,
        [shape(share, part)],
        (held, own, ring(low, -1), ring(high, 1), ring(opposite, 2), gate_table),
    )

    (velocity,) = small_call(
        velocity_kernel, [smem()] + [vmem()] * 6, [shape(rows, part)], (facts, p_own, *last, latents, gate_table)
    )
    return (velocity, head_frame)


def solution(mesh):
    placed = (
        P("queue", "mp"),
        P("queue"),
        P(),
        P("mp"),
        P(),
        P(None, "mp"),
        P(None, None, "mp"),
        P("mp", None),
    )
    return jax.shard_map(
        on_device,
        mesh=mesh,
        in_specs=placed,
        out_specs=(P("queue", "mp"), P("queue", "mp")),
        check_vma=False,
    )
```

```python
import functools

import jax
import jax.numpy as jnp
from jax import lax
from jax.experimental import pallas as pl
from jax.experimental.pallas import tpu as pltpu
from jax.sharding import PartitionSpec as P

STEPS = 50
EPS = 1e-06
BIG = 1e30
SEEN, WINDOW, HEAD, OWN_STEP, MARKS = 8, 68, 70, 73, 75
LOG2E = 1.4426950408889634
VMEM_LIMIT = 48 * 1024 * 1024
SMALL_LIMIT = 12 * 1024 * 1024


def ring(value, distance):
    return lax.ppermute(value, "mp", [(s, s // 4 * 4 + (s + distance) % 4) for s in range(8)])


def across(value):
    return lax.ppermute(value, "mp", [(s, s ^ 4) for s in range(8)])


def shifted(value, distance):
    count = lax.axis_size("queue")
    return lax.ppermute(value, "queue", [(s, (s + distance) % count) for s in range(count)])


def flipped(value, bit):
    return lax.ppermute(value, "queue", [(s, s ^ bit) for s in range(lax.axis_size("queue"))])


def vmem():
    return pl.BlockSpec(memory_space=pltpu.VMEM)


def anywhere():
    return pl.BlockSpec(memory_space=pl.ANY)


def smem():
    return pl.BlockSpec(memory_space=pltpu.SMEM)


def product_kernel(first, place, own_at, far, low, high, far_opp, two_a, two_b, two_c, modul, weight_at, out, made, own, weight, sems):
    rows, part = own.shape
    half = rows // 2
    width = weight.shape[0]
    cut = two_a.shape[0] - half
    copies = [
        pltpu.make_async_copy(source, target, sems.at[i])
        for i, (source, target) in enumerate(((own_at, own), *((weight_at.at[first + which], weight.at[:, which * part : (which + 1) * part]) for which in range(out.shape[0]))))
    ]
    for copy in copies:
        copy.start()
    copies[0].wait()
    starts = [pl.multiple_of(place[i] * part, 128) for i in range(8)]
    chunk = 32
    for frame in range(2):
        for at in range(frame * half, (frame + 1) * half, chunk):
            parts = [
                (own, at), (far, at), (low, at), (high, at),
                (two_a, at) if at < half else (two_b, at - half),
                (two_a, half + at) if at < cut else (two_c, at - cut),
                (two_c, rows - cut + at) if at < rows - cut else (two_b, half + at - (rows - cut)),
                (far_opp, at),
            ]

            def load(i):
                ref, base = parts[i]
                return ref[base : base + chunk, :].astype(jnp.float32)

            total = load(0)
            for i in range(1, 8):
                total = total + load(i)
            mean = jnp.sum(total, axis=1, keepdims=True) * (1.0 / width)
            square = jnp.square(load(0) - mean)
            for i in range(1, 8):
                square = square + jnp.square(load(i) - mean)
            var = jnp.sum(square, axis=1, keepdims=True) * (1.0 / width)
            inverse = lax.rsqrt(var + EPS)
            for i in range(8):
                columns = pl.ds(starts[i], part)
                shift = modul[frame, 0:1, columns].astype(jnp.float32)
                scale = modul[frame, 1:2, columns].astype(jnp.float32) + 1.0
                value = (load(i) - mean) * inverse * scale + shift
                made[at : at + chunk, columns] = value.astype(jnp.bfloat16)
    for copy in copies[1:]:
        copy.wait()
    result = jnp.dot(made[...], weight[...], preferred_element_type=jnp.float32).astype(jnp.bfloat16)
    for which in range(out.shape[0]):
        for h in range(3):
            at = which * part + h * 128
            out[which, h] = result[:, at : at + 128]


def products(first, count, heads, facts, latents, blocks, modul, weight):
    rows, part = latents.shape
    width = weight.shape[1]
    bf = jnp.bfloat16
    return pl.pallas_call(
        functools.partial(product_kernel, first),
        out_shape=jax.ShapeDtypeStruct((count, heads, rows, part // heads), bf),
        in_specs=[smem(), anywhere()] + [vmem()] * 8 + [anywhere()],
        out_specs=vmem(),
        scratch_shapes=[
            pltpu.VMEM((rows, width), bf),
            pltpu.VMEM((rows, part), bf),
            pltpu.VMEM((width, count * part), bf),
            pltpu.SemaphoreType.DMA((1 + count,)),
        ],
        compiler_params=pltpu.CompilerParams(vmem_limit_bytes=VMEM_LIMIT),
        cost_estimate=pl.CostEstimate(flops=2 * count * rows * width * part, bytes_accessed=2 * (count + 1) * width * part, transcendentals=0),
    )(facts, latents, *blocks, modul, weight)


def attend_kernel(shape, allowed, query, *rest):
    blocks, first, last = shape
    keys, rest = rest[: len(blocks)], rest[len(blocks) :]
    if not first:
        top_in, sum_in, *rest = rest
    if last:
        out, scores = rest
    else:
        top_out, sum_out, scores = rest
    size = query.shape[2]
    tokf = query.shape[1] // 2
    factor = LOG2E / size**0.5
    ones = jnp.ones((tokf, size), jnp.bfloat16)
    for head, f in [(head, f) for head in range(query.shape[0]) for f in range(2)]:
        rows = slice(f * tokf, (f + 1) * tokf)
        q = query[head, rows, :]
        tiles = []
        for ref, slot in zip(keys, blocks):
            for g in range(2):
                if (slot, g, f) in ((0, 0, 1), (4, 1, 0)):
                    continue
                place = allowed[WINDOW + slot - 5] if slot >= 5 else slot
                tiles.append((ref, slice(g * tokf, (g + 1) * tokf), allowed[SEEN + (head * 2 + f) * 10 + place * 2 + g] > 0))
        top = jnp.full((tokf, size), -BIG, jnp.float32)
        for t, (ref, at, seen) in enumerate(tiles):
            s = lax.dot_general(q, ref[0, head, at, :], (((1,), (1,)), ((), ())), preferred_element_type=jnp.float32)
            scores[(head + f) % 2, t] = s
            top = jnp.maximum(top, jnp.where(seen, jnp.maximum(s[:, :size], s[:, size:]), -BIG))
        largest = jnp.broadcast_to(jnp.max(top, axis=1, keepdims=True) * factor, (tokf, size))
        total = jnp.zeros((tokf, 2 * size), jnp.float32)
        if not first:
            before = top_in[head, rows, :]
            largest = jnp.maximum(largest, before)
            fade = jnp.exp2(before - largest)
            total = sum_in[head, rows, :] * jnp.concatenate([fade, fade], axis=1)
        for t, (ref, at, seen) in enumerate(tiles):
            v = jnp.concatenate([ref[1, head, at, :], ones], axis=1)
            base = jnp.where(seen, largest, BIG)
            weights = jnp.concatenate(
                [jnp.exp2(scores[(head + f) % 2, t, :, i * size : (i + 1) * size] * factor - base) for i in range(2)], axis=1
            ).astype(jnp.bfloat16)
            total = total + jnp.dot(weights, v, preferred_element_type=jnp.float32)
        if last:
            out[rows, head * size : (head + 1) * size] = (total[:, :size] / total[:, size:]).astype(jnp.bfloat16)
        else:
            top_out[head, rows, :] = largest
            sum_out[head, rows, :] = total


def attend(blocks, allowed, query, keys, state=(), last=False):
    heads, rows, size = query.shape
    tokf = rows // 2
    if last:
        out_shape = jax.ShapeDtypeStruct((rows, heads * size), jnp.bfloat16)
    else:
        out_shape = [jax.ShapeDtypeStruct((heads, rows, n * size), jnp.float32) for n in (1, 2)]
    tiles = 4 * len(blocks)
    return pl.pallas_call(
        functools.partial(attend_kernel, (blocks, not state, last)),
        out_shape=out_shape,
        in_specs=[smem()] + [vmem()] * (1 + len(keys) + len(state)),
        out_specs=vmem() if last else [vmem()] * 2,
        scratch_shapes=[pltpu.VMEM((2, 2 * len(blocks), tokf, tokf), jnp.float32)],
        compiler_params=pltpu.CompilerParams(vmem_limit_bytes=SMALL_LIMIT),
        cost_estimate=pl.CostEstimate(
            flops=6 * heads * tiles * tokf * tokf * size, bytes_accessed=4 * tiles * tokf * size, transcendentals=heads * tiles * tokf * tokf
        ),
    )(allowed, query, *keys, *state)


def added(*terms):
    total = terms[0].astype(jnp.float32)
    for term in terms[1:]:
        total = total + term.astype(jnp.float32)
    return total


def product(place, slots, left, weight):
    part = weight.shape[0]
    columns = [weight[:, pl.ds(pl.multiple_of(place[slot] * part, 128), part)] for slot in slots]
    result = jnp.dot(left, jnp.concatenate(columns, axis=1), preferred_element_type=jnp.float32).astype(jnp.bfloat16)
    return [result[:, i * part : (i + 1) * part] for i in range(len(slots))]


def first_kernel(cut, place, attended, weight, far_opp, two_a, two_b, two_c):
    rows = attended.shape[0]
    half = rows // 2
    left = attended[...]
    far_opp[...], opp = product(place, (7, 4), left, weight)
    far_low, far_high = product(place, (5, 6), left, weight)
    two_a[:half] = opp[:half]
    two_a[half:] = far_low[:cut]
    two_b[:half] = opp[half:]
    two_b[half:] = far_high[rows - cut :]
    two_c[: rows - cut] = far_low[cut:]
    two_c[rows - cut :] = far_high[: rows - cut]


def second_kernel(cut, place, attended, weight, got_opp, got_a, got_b, got_c, sum_far, sum_low, sum_high, own):
    rows = attended.shape[0]
    half = rows // 2
    bf = jnp.bfloat16
    left = attended[...]
    far, low = product(place, (1, 2), left, weight)
    high, own[...] = product(place, (3, 0), left, weight)
    sum_far[:cut] = added(far[:cut], got_opp[:cut], got_a[half:]).astype(bf)
    sum_far[cut : rows - cut] = added(far[cut : rows - cut], got_opp[cut : rows - cut]).astype(bf)
    sum_far[rows - cut :] = added(far[rows - cut :], got_opp[rows - cut :], got_b[half:]).astype(bf)
    sum_low[:cut] = added(low[:cut], got_a[:cut]).astype(bf)
    sum_low[cut:half] = added(low[cut:half], got_a[cut:half], got_c[: half - cut]).astype(bf)
    sum_low[half:] = added(low[half:], got_c[half - cut : rows - cut]).astype(bf)
    sum_high[:half] = added(high[:half], got_c[rows - cut : rows - cut + half]).astype(bf)
    sum_high[half : rows - cut] = added(high[half : rows - cut], got_b[: half - cut], got_c[rows - cut + half :]).astype(bf)
    sum_high[rows - cut :] = added(high[rows - cut :], got_b[half - cut : half]).astype(bf)


def summed(kernel, place, attended, weight, terms, heights):
    rows, part = attended.shape
    return pl.pallas_call(
        kernel,
        out_shape=[jax.ShapeDtypeStruct((height, part), jnp.bfloat16) for height in heights],
        in_specs=[smem()] + [vmem()] * (2 + len(terms)),
        out_specs=[vmem()] * len(heights),
        compiler_params=pltpu.CompilerParams(vmem_limit_bytes=SMALL_LIMIT),
        cost_estimate=pl.CostEstimate(flops=8 * rows * part * part, bytes_accessed=18 * rows * part, transcendentals=0),
    )(place, attended, weight, *terms)


def split_kernel(at, marks, kept, got, send, keep):
    mine = marks[at + 1]
    for i in range(send.shape[0]):
        for out, side in ((send, 1 - mine), (keep, mine)):
            row = 2 * i + side
            out[i] = jnp.where(marks[at] > 0, kept[row].astype(jnp.float32), got[row].astype(jnp.float32)).astype(jnp.bfloat16)


def split(step, facts, kept, got):
    count, share, columns = kept.shape
    return pl.pallas_call(
        functools.partial(split_kernel, MARKS + 2 * step),
        out_shape=[jax.ShapeDtypeStruct((count // 2, share, columns), jnp.bfloat16)] * 2,
        in_specs=[smem(), vmem(), vmem()],
        out_specs=[vmem()] * 2,
        compiler_params=pltpu.CompilerParams(vmem_limit_bytes=SMALL_LIMIT),
        cost_estimate=pl.CostEstimate(flops=count * share * columns, bytes_accessed=6 * count * share * columns, transcendentals=0),
    )(facts, kept, got)


def turned(index):
    return index ^ (((index >> 3) & 1) << 2)


def head_kernel(marks, attended, latents, send, keep, scratch):
    part = attended.shape[1]
    tokf = scratch.shape[0]
    rows = pl.ds(pl.multiple_of(marks[HEAD] * tokf, tokf), tokf)
    scratch[:, :part] = attended[rows, :].astype(jnp.float32)
    scratch[:, part : 2 * part] = latents[rows, :].astype(jnp.float32)
    scratch[:, 2 * part :] = jnp.full((tokf, scratch.shape[1] - 2 * part), marks[HEAD + 2].astype(jnp.float32))
    share = send.shape[1]
    for i in range(send.shape[0]):
        for out, side in ((send, 1 - marks[HEAD + 1]), (keep, marks[HEAD + 1])):
            row = pl.multiple_of((turned(2 * i) + side) * share, share)
            out[i] = scratch[pl.ds(row, share), :].astype(jnp.bfloat16)


def share_kernel(place, kept, got, weight, rows, own, far):
    part = weight.shape[0]
    chosen = jnp.where(place[MARKS + 8] > 0, kept[0].astype(jnp.float32), got[0].astype(jnp.float32))
    rows[...] = chosen
    left = jnp.concatenate([chosen[:, :part]] * 2, axis=0).astype(jnp.bfloat16)
    for out, slots in ((own, (0, 2, 3, 4)), (far, (1, 5, 6, 7))):
        for i, slot in enumerate(slots):
            columns = pl.ds(pl.multiple_of(place[slot] * part, 128), part)
            result = jnp.dot(left, weight[:, columns], preferred_element_type=jnp.float32)
            out[i] = result[: out.shape[1]].astype(jnp.bfloat16)


def pass_kernel(own, far, *outs):
    for i, out in enumerate(outs):
        out[...] = added(own[i], far[i]).astype(jnp.bfloat16)


def estimate_kernel(rows, own, low, high, opposite, gates, out):
    part = own.shape[1]
    latent = rows[:, part : 2 * part]
    step = rows[0:1, 2 * part : 2 * part + 1]
    index = lax.broadcasted_iota(jnp.int32, gates.shape, 0).astype(jnp.float32) + 1.0
    gate = jnp.sum(jnp.where(index == step, gates[...].astype(jnp.float32), 0.0), axis=0, keepdims=True)
    velocity = (latent + gate * added(own[...], low[...], high[...], opposite[...])).astype(jnp.bfloat16)
    level = step / STEPS
    sigma = 3.0 * level / (1.0 + 2.0 * level)
    out[...] = (latent - sigma * velocity.astype(jnp.float32)).astype(jnp.bfloat16)


def velocity_kernel(facts, own, far, low, high, latents, gates, velocity):
    tokf = own.shape[0] // 2
    index = lax.broadcasted_iota(jnp.int32, gates.shape, 0) + 1
    for frame in range(2):
        at = slice(frame * tokf, (frame + 1) * tokf)
        gate = jnp.sum(jnp.where(index == facts[OWN_STEP + frame], gates[...].astype(jnp.float32), 0.0), axis=0, keepdims=True)
        projected = added(own[at, :], far[at, :], low[at, :], high[at, :])
        velocity[at, :] = (latents[at, :].astype(jnp.float32) + gate * projected).astype(jnp.bfloat16)


def small_call(kernel, in_specs, shapes, args, scratch=()):
    return pl.pallas_call(
        kernel,
        out_shape=shapes,
        in_specs=in_specs,
        out_specs=[vmem()] * len(shapes),
        scratch_shapes=list(scratch),
        compiler_params=pltpu.CompilerParams(vmem_limit_bytes=SMALL_LIMIT),
        cost_estimate=pl.CostEstimate(flops=1 << 20, bytes_accessed=1 << 20, transcendentals=0),
    )(*args)


def on_device(latents, step_index, head_index, band, mod_table, gate_table, qkv_weight, out_weight):
    rows, part = latents.shape
    frames = step_index.shape[0]
    tokf = rows // frames
    width = mod_table.shape[2]
    heads = band.shape[0]
    size = part // heads
    count = lax.axis_size("queue")
    me = lax.axis_index("queue")
    member = lax.axis_index("mp")
    frames_all = frames * count
    half = rows // 2
    x, y = member & 3, member >> 2
    slots = [yy * 4 + xx for yy, xx in (
        (y, x), (1 - y, x), (y, (x + 3) & 3), (y, (x + 1) & 3),
        (y, x ^ 2), (1 - y, (x + 3) & 3), (1 - y, (x + 1) & 3), (1 - y, x ^ 2),
    )]
    odd = me & 1 == 1
    head = head_index[0]
    position = (me * frames + jnp.arange(frames, dtype=jnp.int32) - head) & (frames_all - 1)
    offset = jnp.arange(5 * frames, dtype=jnp.int32)[None, :] - 2 * frames - jnp.arange(frames, dtype=jnp.int32)[:, None]
    other = position[:, None] + offset
    inside = (other >= 0) & (other < frames_all)
    near = jnp.abs(offset)[None, :, :] <= band[:, None, None]
    allowed = (inside[None, :, :] & near).reshape(-1)
    local_frame = head & 1
    mine, source = turned(me), turned(head >> 1)
    small = [jnp.where(odd, 1, 3), jnp.where(odd, 3, 1), local_frame, me & 1, lax.dynamic_index_in_dim(step_index, local_frame, 0, keepdims=False)]
    small += [step_index[f] for f in range(frames)]
    for bit in (1, 2, 4, 8, 16):
        small += [((source ^ mine) & bit) == 0, (mine & (2 * bit)) != 0]
    facts = jnp.concatenate([jnp.stack([jnp.asarray(v, jnp.int32) for v in slots]), allowed.astype(jnp.int32), jnp.stack([jnp.asarray(v, jnp.int32) for v in small])])

    cut = 64
    bf = jnp.bfloat16
    far, low, high = across(latents), ring(latents, 1), ring(latents, -1)
    far_opp = ring(far, 2)
    two_a = ring(jnp.concatenate([low[:half], far[:cut]]), 1)
    two_b = ring(jnp.concatenate([high[half:], far[rows - cut :]]), -1)
    two_c = across(jnp.concatenate([low[cut:], high[: rows - cut]]))

    modul = jnp.concatenate([lax.dynamic_index_in_dim(mod_table, step_index[f] - 1, 0) for f in range(frames)])
    blocks = (far, low, high, far_opp, two_a, two_b, two_c)
    kv = products(1, 2, heads, facts, latents, blocks, modul, qkv_weight)

    upper2 = shifted(kv, -2)
    lower2 = shifted(kv, 2)
    partner = flipped(kv, 1)
    query = products(0, 1, heads, facts, latents, blocks, modul, qkv_weight)[0]

    state = attend((2, 5), facts, query, (kv, partner))
    upper2, lower2, *state = lax.optimization_barrier((upper2, lower2, *state))
    passed = flipped(jnp.where(odd, lower2, upper2), 1)
    state = attend((4, 0), facts, query, (upper2, lower2), state)
    attended = attend((6,), facts, query, (passed,), state, last=True)

    sent_opp, two_a, two_b, two_c = summed(
        functools.partial(first_kernel, cut), facts, attended, out_weight, (), (rows, half + cut, half + cut, 2 * (rows - cut))
    )
    got = ring(sent_opp, 2), ring(two_a, -1), ring(two_b, 1), across(two_c)

    share = tokf // count
    wide = 2 * part + 128

    def shape(*dims, kind=bf):
        return jax.ShapeDtypeStruct(dims, kind)

    send, kept = small_call(
        head_kernel,
        [smem()] + [vmem()] * 2,
        [shape(count // 2, share, wide)] * 2,
        (facts, lax.optimization_barrier((attended, sent_opp))[0], latents),
        [pltpu.VMEM((tokf, wide), jnp.float32)],
    )
    moved = flipped(send, 1)
    for step in (0, 1, 2):
        send, kept = split(step, facts, kept, moved)
        moved = flipped(send, turned(2 << step))
    *got, moved = lax.optimization_barrier((*got, moved))
    sum_far, sum_low, sum_high, p_own = summed(functools.partial(second_kernel, cut), facts, attended, out_weight, got, (rows,) * 4)
    last = across(sum_far), ring(sum_low, -1), ring(sum_high, 1)
    send, kept = split(3, facts, kept, moved)
    moved = flipped(send, 16)
    held, mini_own, mini_far = small_call(
        share_kernel,
        [smem()] + [vmem()] * 3,
        [shape(share, wide, kind=jnp.float32)] + [shape(4, share, part)] * 2,
        (facts, kept, moved, out_weight),
    )
    *last, mini_far = lax.optimization_barrier((*last, across(mini_far)))
    own, low, high, opposite = small_call(pass_kernel, [vmem()] * 2, [shape(share, part)] * 4, (mini_own, mini_far))
    (head_frame,) = small_call(
        estimate_kernel,
        [vmem()] * 6,
        [shape(share, part)],
        (held, own, ring(low, -1), ring(high, 1), ring(opposite, 2), gate_table),
    )

    (velocity,) = small_call(
        velocity_kernel, [smem()] + [vmem()] * 6, [shape(rows, part)], (facts, p_own, *last, latents, gate_table)
    )
    return (velocity, head_frame)


def solution(mesh):
    placed = (
        P("queue", "mp"),
        P("queue"),
        P(),
        P("mp"),
        P(),
        P(None, "mp"),
        P(None, None, "mp"),
        P("mp", None),
    )
    return jax.shard_map(
        on_device,
        mesh=mesh,
        in_specs=placed,
        out_specs=(P("queue", "mp"), P("queue", "mp")),
        check_vma=False,
    )
```
